32 devices in a mesh: groups: 2 (over y), seq: 4 (over z), tensor: 4 (over x, core).
Axes of the slice: x: 2, y: 2, z: 4, core: 2. Of those that a mesh axis runs over, the one named last changes fastest.
Arguments:
- video_query: bfloat16 [1024, 4096], P(('groups', 'seq'), 'tensor'), parts along dimension 0, may hold values from -21 to 21
- video_key: bfloat16 [1024, 4096], P(('groups', 'seq'), 'tensor'), parts along dimension 0, may hold values from -21 to 21
- video_value: bfloat16 [1024, 4096], P(('groups', 'seq'), 'tensor'), parts along dimension 0, may hold values from -6 to 6
- video_stream: bfloat16 [1024, 4096], P(('groups', 'seq'), 'tensor'), parts along dimension 0, may hold values from -6 to 6
- out_weight: bfloat16 [4096, 4096], P('tensor'), may hold values from -0.09375 to 0.09375
- cross_query: bfloat16 [1024, 2048], P(('groups', 'seq'), 'tensor'), parts along dimension 0, may hold values from -21 to 21
- audio_key: bfloat16 [128, 2048], P(('groups', 'seq'), 'tensor'), parts along dimension 0, may hold values from -21 to 21
- audio_value: bfloat16 [128, 2048], P(('groups', 'seq'), 'tensor'), parts along dimension 0, may hold values from -6 to 6
- audio_query: bfloat16 [128, 2048], P(('groups', 'seq'), 'tensor'), parts along dimension 0, may hold values from -21 to 21
- cross_key: bfloat16 [1024, 2048], P(('groups', 'seq'), 'tensor'), parts along dimension 0, may hold values from -21 to 21
- cross_value: bfloat16 [1024, 2048], P(('groups', 'seq'), 'tensor'), parts along dimension 0, may hold values from -6 to 6
Outputs:
- video_next: bfloat16 [1024, 4096], P(('groups', 'seq'), 'tensor'), parts along dimension 0
- video_cross: bfloat16 [1024, 2048], P(('groups', 'seq'), 'tensor'), parts along dimension 0
- audio_cross: bfloat16 [128, 2048], P(('groups', 'seq'), 'tensor'), parts along dimension 0
The draws below stay inside these ranges and needn't reach their ends.
There are 2 independent parts, one for each index of `groups`. The reference program is written for one: setup_inputs(seed, part) draws one part's arguments, and reference() takes and returns one part's arrays. A program takes and returns all parts, laid end to end along the dimension named above; an argument that names none is the same for every part. Nothing has to cross between parts.
All inputs are finite; a program needn't handle non-finite values.
Results may differ from the reference program's by a relative error of at most 0.012.
Values may be sent and summed in bfloat16 or wider, within the bound.
No kernel may reach another device: no remote copies, remote signals or barrier semaphores. Data moves between devices by JAX's collectives and lax.ppermute only.
A program may use at most 64 MiB of HBM per device.

```python
import math
import jax
import jax.numpy as jnp
from jax import lax

DV = 4096
DA = 2048
HV = 32
HA = 16
HD = 128
VT = 512
AT = 64


def paired(key, query_rows, key_rows, width, salt):
    subkeys = jax.random.split(jax.random.fold_in(key, salt), 2)
    queries = jnp.clip(1.5 * jax.random.normal(subkeys[0], (query_rows, width), jnp.float32), -6.0, 6.0)
    keyset = jnp.clip(1.5 * jax.random.normal(subkeys[1], (key_rows, width), jnp.float32), -6.0, 6.0)
    return (queries, keyset)


def draw_video_query(key, part):
    return paired(key, VT, VT, DV, 11)[0].astype(jnp.bfloat16)


def draw_video_key(key, part):
    return paired(key, VT, VT, DV, 11)[1].astype(jnp.bfloat16)


def draw_cross_query(key, part):
    return paired(key, VT, AT, DA, 23)[0].astype(jnp.bfloat16)


def draw_audio_key(key, part):
    return paired(key, VT, AT, DA, 23)[1].astype(jnp.bfloat16)


def draw_audio_query(key, part):
    return paired(key, AT, VT, DA, 37)[0].astype(jnp.bfloat16)


def draw_cross_key(key, part):
    return paired(key, AT, VT, DA, 37)[1].astype(jnp.bfloat16)


def block_levels(stream_key, shape, pieces, low, largest):
    def one(position, shards_of):
        heights = jax.random.uniform(jax.random.fold_in(jax.random.fold_in(stream_key, 6), position), (shards_of,), jnp.float32, low / len(pieces), largest / len(pieces))
        return jnp.repeat(jnp.exp(heights), shape[position] // shards_of).reshape((-1,) + (1,) * (len(shape) - position - 1))

    factor_of = one(*pieces[0])
    for cut in pieces[1:]:
        factor_of = factor_of * one(*cut)
    return factor_of


def bell_draw(key, dims, spread, limit, pieces=(), held_as=jnp.bfloat16):
    entries = spread * jax.random.normal(key, dims, jnp.float32)
    if pieces:
        entries = entries * block_levels(key, dims, pieces, -0.22, 0.18)
    return jnp.clip(entries, -limit, limit).astype(held_as)


def setup_inputs(seed: int = 0, part: int = 0) -> dict:
    arg_keys = jax.random.split(jax.random.key(seed), 12)
    part_keys = jax.random.split(jax.random.fold_in(arg_keys[11], part), 12)
    return {
        "video_query": draw_video_query(jax.random.fold_in(jax.random.fold_in(arg_keys[11], part), 71), part),
        "video_key": draw_video_key(jax.random.fold_in(jax.random.fold_in(arg_keys[11], part), 71), part),
        "video_value": bell_draw(part_keys[2], (VT, DV), 1.0, 6.0, ((0, 4), (1, 4))),
        "video_stream": bell_draw(part_keys[3], (VT, DV), 1.0, 6.0, ((0, 4), (1, 4))),
        "out_weight": bell_draw(arg_keys[4], (DV, DV), DV ** -0.5, 0.09375, ((0, 4),)),
        "cross_query": draw_cross_query(jax.random.fold_in(jax.random.fold_in(arg_keys[11], part), 71), part),
        "audio_key": draw_audio_key(jax.random.fold_in(jax.random.fold_in(arg_keys[11], part), 71), part),
        "audio_value": bell_draw(part_keys[7], (AT, DA), 1.0, 6.0, ((0, 4), (1, 4))),
        "audio_query": draw_audio_query(jax.random.fold_in(jax.random.fold_in(arg_keys[11], part), 71), part),
        "cross_key": draw_cross_key(jax.random.fold_in(jax.random.fold_in(arg_keys[11], part), 71), part),
        "cross_value": bell_draw(part_keys[10], (VT, DA), 1.0, 6.0, ((0, 4), (1, 4))),
    }


def attend(queries, keyset, values, head_count):
    query_rows = queries.shape[0]
    key_rows = keyset.shape[0]
    query_head = queries.reshape(query_rows, head_count, HD).transpose(1, 0, 2)
    key_head = keyset.reshape(key_rows, head_count, HD).transpose(1, 0, 2)
    value_head = values.reshape(key_rows, head_count, HD).transpose(1, 0, 2)

    def single(operands):
        query_one, key_one, value_one = operands
        scores = jnp.dot(query_one, key_one.T, preferred_element_type=jnp.float32) * (1.0 / math.sqrt(HD))
        row_max = lax.optimization_barrier(jnp.max(scores, axis=1, keepdims=True))
        raised = jnp.exp(scores - row_max)
        row_sum = lax.optimization_barrier(jnp.sum(raised, axis=1, keepdims=True))
        weights = raised.astype(jnp.bfloat16)
        return jnp.dot(weights, value_one, preferred_element_type=jnp.float32) / row_sum
    result = lax.map(single, (query_head, key_head, value_head))
    return result.transpose(1, 0, 2).reshape(query_rows, head_count * HD)

def reference(video_query, video_key, video_value, video_stream, out_weight, cross_query, audio_key, audio_value, audio_query, cross_key, cross_value):
    video_heads = attend(video_query, video_key, video_value, HV).astype(jnp.bfloat16)
    projected = jnp.dot(video_heads, out_weight, preferred_element_type=jnp.float32)
    video_next = (video_stream.astype(jnp.float32) + projected).astype(jnp.bfloat16)
    video_cross = attend(cross_query, audio_key, audio_value, HA).astype(jnp.bfloat16)
    audio_cross = attend(audio_query, cross_key, cross_value, HA).astype(jnp.bfloat16)
    return (video_next, video_cross, audio_cross)
```

```python
import functools
import math

import jax
import jax.numpy as jnp
from jax import lax
from jax.experimental import pallas as pl
from jax.experimental.pallas import tpu as pltpu
from jax.sharding import PartitionSpec as P

HD = 128
FACTOR = 1.0 / math.sqrt(HD)
LOG2E = math.log2(math.e)
BF16 = jnp.bfloat16
F32 = jnp.float32
MIB = 1 << 20
ANY = pl.BlockSpec(memory_space=pl.ANY)
VM = pl.BlockSpec(memory_space=pltpu.VMEM)


def rows_of(total, size):
    return [slice(start, start + size) for start in range(0, total, size)]


def partner(axis, size, mask):
    return functools.partial(
        lax.ppermute, axis_name=axis, perm=[(i, i ^ mask) for i in range(size)]
    )


def pack_kernel(count, q, k, v, ak, av, aq, *rest):
    outs, audio, sem = rest[:count], rest[count], rest[count + 1]
    rows, width = q.shape[0], q.shape[1] // count
    arows = ak.shape[0]
    z = lax.axis_index("seq")
    copies = []
    for mask in range(count):
        owner = jnp.bitwise_xor(z, mask)
        columns = pl.ds(pl.multiple_of(owner * width, width), width)
        for position, source in enumerate((q, k, v)):
            copies.append(
                pltpu.make_async_copy(
                    source.at[:, columns],
                    outs[mask].at[pl.ds(position * rows, rows)],
                    sem.at[len(copies)],
                )
            )
    for position, source in enumerate((ak, av, aq)):
        copies.append(
            pltpu.make_async_copy(
                source, audio.at[pl.ds(position * arows, arows)], sem.at[len(copies)]
            )
        )
    for copy in copies:
        copy.start()
    for copy in copies:
        copy.wait()


def pack(count, q, k, v, ak, av, aq):
    rows, width = q.shape[0], q.shape[1] // count
    arows = ak.shape[0]
    return pl.pallas_call(
        functools.partial(pack_kernel, count),
        out_shape=[jax.ShapeDtypeStruct((3 * rows, width), BF16)] * count
        + [jax.ShapeDtypeStruct((3 * arows, ak.shape[1]), BF16)],
        in_specs=[ANY] * 6,
        out_specs=[ANY] * (count + 1),
        scratch_shapes=[pltpu.SemaphoreType.DMA((3 * count + 3,))],
        compiler_params=pltpu.CompilerParams(vmem_limit_bytes=1 * MIB),
        name="pack",
    )(q, k, v, ak, av, aq)


def softmax_times(scores, value):
    highest = jnp.max(scores, axis=1, keepdims=True)
    raised = jnp.exp2(scores * (FACTOR * LOG2E) - highest * (FACTOR * LOG2E))
    total = jnp.sum(raised, axis=1, keepdims=True)
    numerator = jnp.dot(raised.astype(BF16), value, preferred_element_type=F32)
    return highest, total, numerator


def nt(a, b):
    return lax.dot_general(a, b, (((1,), (1,)), ((), ())), preferred_element_type=F32)


def attend_kernel(count, *refs):
    packs, outs = refs[:count], refs[count:]
    rows = packs[0].shape[0] // 3
    for columns in rows_of(packs[0].shape[1], HD):
        key = jnp.concatenate([p[rows : 2 * rows, columns] for p in packs], axis=0)
        value = jnp.concatenate([p[2 * rows :, columns] for p in packs], axis=0)
        for pack_ref, out in zip(packs, outs):
            _, total, numerator = softmax_times(nt(pack_ref[:rows, columns], key), value)
            out[:, columns] = (numerator / total).astype(BF16)


def attend(packs):
    count = len(packs)
    rows, width = packs[0].shape[0] // 3, packs[0].shape[1]
    return pl.pallas_call(
        functools.partial(attend_kernel, count),
        out_shape=[jax.ShapeDtypeStruct((rows, width), BF16)] * count,
        in_specs=[VM] * count,
        out_specs=[VM] * count,
        compiler_params=pltpu.CompilerParams(vmem_limit_bytes=12 * MIB),
        name="attend",
    )(*packs)


def fetch_kernel(w, out, sem):
    copy = pltpu.make_async_copy(w, out, sem)
    copy.start()
    copy.wait()


def fetch(w):
    return pl.pallas_call(
        fetch_kernel,
        out_shape=pltpu.VMEM(w.shape, w.dtype),
        in_specs=[ANY],
        out_specs=VM,
        scratch_shapes=[pltpu.SemaphoreType.DMA],
        compiler_params=pltpu.CompilerParams(vmem_limit_bytes=1 * MIB),
        name="fetch",
    )(w)


def project_kernel(count, tensor, *refs):
    heads, w, keep, send, lhs = refs[:count], refs[count], refs[count + 1], refs[count + 2], refs[count + 3]
    width = heads[0].shape[1]
    z = lax.axis_index("seq")
    t = lax.axis_index("tensor")
    for mask in range(count):
        owner = jnp.bitwise_xor(z, mask)
        lhs[:, pl.ds(pl.multiple_of(owner * width, width), width)] = heads[mask][...]
    share = w.shape[1] // tensor
    step = min(512, share)
    for core in (1, 0):
        for mask in range(tensor // 2):
            owner = jnp.bitwise_xor(t, 2 * mask + core)
            for start in range(0, share, step):
                columns = pl.ds(pl.multiple_of(owner * share + start, step), step)
                product = jnp.dot(lhs[...], w[:, columns], preferred_element_type=F32)
                if core:
                    send[mask, :, start : start + step] = product.astype(BF16)
                else:
                    keep[mask, :, start : start + step] = product


def project(heads, w, tensor):
    count = len(heads)
    rows, share = heads[0].shape[0], w.shape[1] // tensor
    return pl.pallas_call(
        functools.partial(project_kernel, count, tensor),
        out_shape=[
            jax.ShapeDtypeStruct((tensor // 2, rows, share), F32),
            jax.ShapeDtypeStruct((tensor // 2, rows, share), BF16),
        ],
        in_specs=[VM] * (count + 1),
        out_specs=[VM] * 2,
        scratch_shapes=[pltpu.VMEM((rows, w.shape[0]), BF16)],
        compiler_params=pltpu.CompilerParams(vmem_limit_bytes=24 * MIB),
        name="project",
    )(*heads, w)


def cross_kernel(count, cq, ck, cv, *refs):
    audios, vc, parts = refs[:count], refs[count], refs[count + 1 :]
    arows = audios[0].shape[0] // 3
    heads = cq.shape[1] // HD
    akey = jnp.concatenate([a[:arows, :] for a in audios], axis=0)
    avalue = jnp.concatenate([a[arows : 2 * arows, :] for a in audios], axis=0)
    aquery = jnp.concatenate([a[2 * arows :, :] for a in audios], axis=0)
    lane = lax.broadcasted_iota(jnp.int32, (count * arows, HD), 1)
    stats = jnp.zeros((count * arows, HD), F32)
    for head in range(heads):
        columns = slice(head * HD, (head + 1) * HD)
        _, total, numerator = softmax_times(nt(cq[:, columns], akey[:, columns]), avalue[:, columns])
        vc[:, columns] = (numerator / total).astype(BF16)
        highest, total, numerator = softmax_times(nt(aquery[:, columns], ck[:, columns]), cv[:, columns])
        partial = (numerator / total).astype(BF16)
        level = highest * (FACTOR * LOG2E) + jnp.log2(total)
        for piece in range(3):
            rounded = level.astype(BF16).astype(F32)
            stats = jnp.where(lane == 3 * head + piece, rounded, stats)
            level = level - rounded
        for index, part in enumerate(parts):
            part[:, columns] = partial[index * arows : (index + 1) * arows]
    for index, part in enumerate(parts):
        part[:, heads * HD :] = stats[index * arows : (index + 1) * arows].astype(BF16)


def cross(cq, ck, cv, audios):
    count = len(audios)
    arows = audios[0].shape[0] // 3
    return pl.pallas_call(
        functools.partial(cross_kernel, count),
        out_shape=[jax.ShapeDtypeStruct(cq.shape, BF16)]
        + [jax.ShapeDtypeStruct((arows, cq.shape[1] + HD), BF16)] * count,
        in_specs=[VM] * (3 + count),
        out_specs=[VM] * (1 + count),
        compiler_params=pltpu.CompilerParams(vmem_limit_bytes=8 * MIB),
        name="cross",
    )(cq, ck, cv, *audios)


def combine_kernel(count, *refs):
    parts, out = refs[:count], refs[count]
    heads = out.shape[1] // HD
    for head in range(heads):
        columns = slice(head * HD, (head + 1) * HD)
        levels = []
        for part in parts:
            pieces = part[:, heads * HD :].astype(F32)[:, 3 * head : 3 * head + 3]
            levels.append(jnp.sum(pieces, axis=1, keepdims=True))
        highest = functools.reduce(jnp.maximum, levels)
        shares = [jnp.exp2(level - highest) for level in levels]
        whole = functools.reduce(jnp.add, shares)
        mixed = functools.reduce(
            jnp.add, [part[:, columns].astype(F32) * share for part, share in zip(parts, shares)]
        )
        out[:, columns] = (mixed / whole).astype(BF16)


def combine(parts):
    count = len(parts)
    shape = (parts[0].shape[0], parts[0].shape[1] - HD)
    return pl.pallas_call(
        functools.partial(combine_kernel, count),
        out_shape=jax.ShapeDtypeStruct(shape, BF16),
        in_specs=[VM] * count,
        out_specs=VM,
        compiler_params=pltpu.CompilerParams(vmem_limit_bytes=2 * MIB),
        name="combine",
    )(*parts)


def exchanged(count, tensor, video_query, video_key, video_value, video_stream, out_weight,
              cross_query, audio_key, audio_value, audio_query, cross_key, cross_value):
    seq = [partner("seq", count, mask) for mask in range(count)]
    masks = list(range(count - 1, 0, -1))
    *packs, audio = pack(count, video_query, video_key, video_value, audio_key, audio_value, audio_query)
    weight = fetch(out_weight)
    for mask in masks:
        packs[mask] = seq[mask](packs[mask])
    heads = attend(packs)
    audios = [audio] + [None] * (count - 1)
    for mask in masks:
        audios[mask] = seq[mask](audio)
    heads = list(heads)
    for mask in masks:
        heads[mask] = seq[mask](heads[mask])
    video_cross, *parts = cross(cross_query, cross_key, cross_value, audios)
    keep, send = project(heads, weight, tensor)
    recv = partner("tensor", tensor, 1)(send)
    total = video_stream.astype(F32) + keep[0] + recv[0].astype(F32)
    for mask in range(1, tensor // 2):
        piece = (keep[mask] + recv[mask].astype(F32)).astype(BF16)
        total = total + partner("tensor", tensor, 2 * mask)(piece).astype(F32)
    video_next = total.astype(BF16)
    for mask in masks:
        parts[mask] = seq[mask](parts[mask])
    return video_next, video_cross, combine(parts)


def blank_state(query_rows, head_count):
    return (
        jnp.full((head_count, query_rows), -1e30, jnp.float32),
        jnp.zeros((head_count, query_rows), jnp.float32),
        jnp.zeros((head_count, query_rows, HD), jnp.float32),
    )


def absorb(carried, queries, keyset, values, head_count):
    running, row_sum, numerator = carried
    query_rows = queries.shape[0]
    key_rows = keyset.shape[0]
    factor = 1.0 / math.sqrt(HD)
    query_heads = queries.reshape(query_rows, head_count, HD)
    for offset in range(0, key_rows, 1024):
        width_keys = min(1024, key_rows - offset)
        key_block = keyset[offset : offset + width_keys].reshape(width_keys, head_count, HD)
        value_block = values[offset : offset + width_keys].reshape(width_keys, head_count, HD)
        scores = (
            jnp.einsum("qhd,khd->hqk", query_heads, key_block, preferred_element_type=jnp.float32)
            * factor
        )
        highest = jnp.maximum(running, jnp.max(scores, axis=2))
        raised = jnp.exp(scores - highest[:, :, None])
        shrink = jnp.exp(running - highest)
        row_sum = row_sum * shrink + jnp.sum(raised, axis=2)
        numerator = numerator * shrink[:, :, None] + jnp.einsum(
            "hqk,khd->hqd",
            raised.astype(jnp.bfloat16),
            value_block,
            preferred_element_type=jnp.float32,
        )
        running = highest
    return (running, row_sum, numerator)


def finish(carried, head_count):
    running, row_sum, numerator = carried
    result = numerator / row_sum[:, :, None]
    return result.transpose(1, 0, 2).reshape(result.shape[1], head_count * HD).astype(jnp.bfloat16)


def gathered(
    video_query,
    video_key,
    video_value,
    video_stream,
    out_weight,
    cross_query,
    audio_key,
    audio_value,
    audio_query,
    cross_key,
    cross_value,
):
    local_heads = video_query.shape[1] // HD
    query_rows = video_query.shape[0]
    pieces = (
        lax.all_gather(video_key, "seq", axis=0, tiled=True),
        lax.all_gather(video_value, "seq", axis=0, tiled=True),
    )
    carried_video = absorb(
        blank_state(query_rows, local_heads), video_query, pieces[0], pieces[1], local_heads
    )
    attended = finish(carried_video, local_heads)
    projected = jnp.dot(attended, out_weight, preferred_element_type=jnp.float32)
    summed = lax.psum_scatter(
        projected.astype(jnp.bfloat16), "tensor", scatter_dimension=1, tiled=True
    ).astype(jnp.float32)
    video_next = (video_stream.astype(jnp.float32) + summed).astype(jnp.bfloat16)
    cross_heads = cross_query.shape[1] // HD
    every_key, every_value = (
        lax.all_gather(audio_key, "seq", axis=0, tiled=True),
        lax.all_gather(audio_value, "seq", axis=0, tiled=True),
    )
    carried_audio = absorb(
        blank_state(cross_query.shape[0], cross_heads),
        cross_query,
        every_key,
        every_value,
        cross_heads,
    )
    video_cross = finish(carried_audio, cross_heads)
    pieces = (
        lax.all_gather(cross_key, "seq", axis=0, tiled=True),
        lax.all_gather(cross_value, "seq", axis=0, tiled=True),
    )
    carried_cross = absorb(
        blank_state(audio_query.shape[0], cross_heads),
        audio_query,
        pieces[0],
        pieces[1],
        cross_heads,
    )
    audio_cross = finish(carried_cross, cross_heads)
    return (video_next, video_cross, audio_cross)


def solution(mesh):
    count, tensor = mesh.shape["seq"], mesh.shape["tensor"]
    both = P(("groups", "seq"), "tensor")
    in_specs = (both,) * 4 + (P("tensor", None),) + (both,) * 6

    def local(*arrays):
        heads = arrays[0].shape[1] // HD
        powers = all(n & (n - 1) == 0 for n in (count, tensor))
        if powers and tensor > 1 and heads % count == 0 and arrays[6].shape[0] % 16 == 0:
            return exchanged(count, tensor, *arrays)
        return gathered(*arrays)

    return jax.shard_map(local, mesh=mesh, in_specs=in_specs, out_specs=(both,) * 3, check_vma=False)
```

```python
import functools
import math

import jax
import jax.numpy as jnp
from jax import lax
from jax.experimental import pallas as pl
from jax.experimental.pallas import tpu as pltpu
from jax.sharding import PartitionSpec as P


HD = 128
FACTOR = 1.0 / math.sqrt(HD)
LOG2E = math.log2(math.e)
BF16 = jnp.bfloat16
F32 = jnp.float32
MIB = 1 << 20
ANY = pl.BlockSpec(memory_space=pl.ANY)
HBM = pl.BlockSpec(memory_space=pltpu.HBM)
VM = pl.BlockSpec(memory_space=pltpu.VMEM)
WHOLE_VMEM = 62.75


COSTS = {"merge": 10000000000, "partials": 3000000000}


def call(kernel, name, shapes, ins, outs, operands, limit, scratch=(), flops=0):
    flops = COSTS.get(name, flops)
    return pl.pallas_call(
        kernel,
        out_shape=shapes,
        in_specs=ins,
        out_specs=outs,
        scratch_shapes=scratch,
        compiler_params=pltpu.CompilerParams(vmem_limit_bytes=int(limit * MIB)),
        cost_estimate=pl.CostEstimate(flops=flops, bytes_accessed=0, transcendentals=0),
        name=name,
    )(*operands)


def partner(axis, size, mask):
    return functools.partial(
        lax.ppermute, axis_name=axis, perm=[(i, i ^ mask) for i in range(size)]
    )


def nt(a, b):
    return lax.dot_general(a, b, (((1,), (1,)), ((), ())), preferred_element_type=F32)


def softmax_times(scores, value):
    highest = jnp.max(scores, axis=1, keepdims=True)
    raised = jnp.exp2(scores * (FACTOR * LOG2E) - highest * (FACTOR * LOG2E))
    total = jnp.sum(raised, axis=1, keepdims=True)
    numerator = jnp.dot(raised.astype(BF16), value, preferred_element_type=F32)
    return highest, total, numerator


def pack_kernel(masks, count, audio_mask, q, k, v, ak, av, aq, *rest):
    own_audio = rest[-2] if audio_mask in masks else None
    outs, sem = rest[-1 - len(masks) - (own_audio is not None) :], rest[-1]
    rows, arows = q.shape[0], aq.shape[0]
    width = q.shape[1] // count
    z = lax.axis_index("seq")
    copies = []

    def copy(source, target):
        copies.append(pltpu.make_async_copy(source, target, sem.at[len(copies)]))
        copies[-1].start()

    for mask, out in zip(masks, outs):
        columns = pl.ds(pl.multiple_of(jnp.bitwise_xor(z, mask) * width, width), width)
        for position, source in enumerate((q, k, v)):
            copy(source.at[:, columns], out.at[pl.ds(position * rows, rows)])
    if own_audio is not None:
        for position, source in enumerate((ak, av, aq)):
            copy(source, own_audio.at[pl.ds(position * arows, arows)])
            for block in range(aq.shape[1] // width if audio_mask else 0):
                copy(
                    source.at[:, pl.ds(block * width, width)],
                    outs[masks.index(audio_mask)].at[pl.ds(3 * rows + (3 * block + position) * arows, arows)],
                )
    for one in copies:
        one.wait()


def pack(masks, count, audio_mask, q, k, v, ak, av, aq, after=()):
    rows, width = q.shape[0], q.shape[1] // count
    below = 3 * aq.size // width
    shapes = [pltpu.VMEM((3 * rows + (below if mask == audio_mask and mask else 0), width), BF16) for mask in masks]
    copies = 3 * len(masks)
    if audio_mask in masks:
        shapes.append(pltpu.VMEM((3 * aq.shape[0], aq.shape[1]), BF16))
        copies += 3 + (3 * aq.shape[1] // width if audio_mask else 0)
    return call(
        functools.partial(pack_kernel, masks, count, audio_mask), "pack", shapes,
        [HBM] * 6 + [ANY] * len(after), [VM] * len(shapes), (q, k, v, ak, av, aq, *after),
        WHOLE_VMEM, [pltpu.SemaphoreType.DMA((copies,))],
    )


def attend_kernel(wanted, order, rows, *refs):
    count = len(order)
    packs, outs = dict(zip(order, refs)), refs[-len(wanted) :]
    for columns in range(0, packs[0].shape[1], HD):
        columns = slice(columns, columns + HD)
        key = jnp.concatenate([p[rows : 2 * rows, columns] for p in packs.values()], axis=0)
        value = jnp.concatenate([p[2 * rows : 3 * rows, columns] for p in packs.values()], axis=0)
        for mask, out in zip(wanted, outs):
            _, total, numerator = softmax_times(nt(packs[mask][:rows, columns], key), value)
            out[:, columns] = (numerator / total).astype(BF16)


def attend(wanted, order, rows, packs, after, name):
    count, width = len(packs), packs[0].shape[1]
    return call(
        functools.partial(attend_kernel, wanted, order, rows), name,
        [jax.ShapeDtypeStruct((rows, width), BF16)] * len(wanted),
        [VM] * count + [ANY] * len(after), [VM] * len(wanted), (*(packs[mask] for mask in order), *after), 8,
        flops=4 * count * len(wanted) * rows * rows * width,
    )


def fetch_kernel(count, *refs):
    copies = [
        pltpu.make_async_copy(refs[i], refs[count + i], refs[-1].at[i]) for i in range(count)
    ]
    for one in copies:
        one.start()
    for one in copies:
        one.wait()


def fetch(*arrays):
    count = len(arrays)
    return call(
        functools.partial(fetch_kernel, count), "fetch", [pltpu.VMEM(x.shape, x.dtype) for x in arrays],
        [HBM] * count, [VM] * count, arrays, 53, [pltpu.SemaphoreType.DMA((count,))],
    )


def project_kernel(order, blocks, step, *refs):
    count = len(order)
    heads, w, lhs = refs[:count], refs[count], refs[-1]
    outs = refs[-1 - len(blocks) : -1]
    width = heads[0].shape[1]
    z = lax.axis_index("seq")
    t = lax.axis_index("tensor")
    for mask, one in zip(order, heads):
        owner = jnp.bitwise_xor(z, mask)
        lhs[:, pl.ds(pl.multiple_of(owner * width, width), width)] = one[...]
    for out, mask in zip(outs, blocks):
        share = out.shape[1]
        owner = jnp.bitwise_xor(t, mask)
        for start in range(0, share, step):
            columns = pl.ds(pl.multiple_of(owner * share + start, step), step)
            product = jnp.dot(lhs[...], w[:, columns], preferred_element_type=F32)
            out[:, start : start + step] = product.astype(out.dtype)


def project(order, heads, w, share, blocks, name, after=()):
    count, rows = len(heads), heads[0].shape[0]
    return call(
        functools.partial(project_kernel, order, list(blocks), math.gcd(512, share)), name,
        [jax.ShapeDtypeStruct((rows, share), dtype) for dtype in blocks.values()],
        [VM] * (count + 1) + [ANY] * len(after), [VM] * len(blocks), (*(heads[mask] for mask in order), w, *after), 8,
        [pltpu.VMEM((rows, w.shape[0]), BF16)],
        flops=2 * rows * w.shape[0] * share * len(blocks),
    )


def stats_of(levels, rows):
    lane = lax.broadcasted_iota(jnp.int32, (rows, HD), 1)
    stats = jnp.zeros((rows, HD), F32)
    for head, level in enumerate(levels):
        for piece in range(3):
            rounded = level.astype(BF16).astype(F32)
            stats = jnp.where(lane == 3 * head + piece, rounded, stats)
            level = level - rounded
    return stats.astype(BF16)


def level_of(stats, head):
    return jnp.sum(stats[:, 3 * head : 3 * head + 3].astype(F32), axis=1, keepdims=True)


def audio_of(audios, audio_mask, first, mask, kind, head):
    arows = audios[0].shape[0] // 3
    ref, at, column = audios[mask], kind * arows, head * HD
    if mask and mask == audio_mask:
        block, column = divmod(column, ref.shape[1])
        at += first + 3 * block * arows
    return ref[at : at + arows, column : column + HD]


def partial_kernel(groups, audio_mask, first, ck, cv, *refs):
    count = sum(size for _, size in groups)
    audios, parts = refs[:count], refs[-len(groups) :]
    arows = audios[0].shape[0] // 3
    heads = ck.shape[1] // HD
    levels = []
    for head in range(heads):
        columns = slice(head * HD, (head + 1) * HD)
        query = jnp.concatenate([audio_of(audios, audio_mask, first, m, 2, head) for m in range(count)], axis=0)
        highest, total, numerator = softmax_times(nt(query, ck[:, columns]), cv[:, columns])
        partial = (numerator / total).astype(BF16)
        levels.append(highest * (FACTOR * LOG2E) + jnp.log2(total))
        for (start, size), part in zip(groups, parts):
            part[:, columns] = partial[start * arows : (start + size) * arows]
    stats = stats_of(levels, count * arows)
    for (start, size), part in zip(groups, parts):
        part[:, heads * HD :] = stats[start * arows : (start + size) * arows]


def partials(groups, audio_mask, first, ck, cv, audios, after):
    count = len(audios)
    arows = audios[0].shape[0] // 3
    return call(
        functools.partial(partial_kernel, groups, audio_mask, first), "partials",
        [jax.ShapeDtypeStruct((size * arows, ck.shape[1] + HD), BF16) for _, size in groups],
        [VM] * (2 + count) + [ANY] * len(after), [VM] * len(groups),
        (ck, cv, *audios, *after), 8, flops=4 * count * arows * ck.size,
    )


def video_cross_kernel(count, audio_mask, first, cq, *refs):
    audios, out = refs[:count], refs[-1]
    for head in range(cq.shape[1] // HD):
        columns = slice(head * HD, (head + 1) * HD)
        key, value = [
            jnp.concatenate([audio_of(audios, audio_mask, first, m, kind, head) for m in range(count)], axis=0)
            for kind in range(2)
        ]
        _, total, numerator = softmax_times(nt(cq[:, columns], key), value)
        out[:, columns] = (numerator / total).astype(BF16)


def crossed(audio_mask, first, cq, audios, after):
    count = len(audios)
    return call(
        functools.partial(video_cross_kernel, count, audio_mask, first), "video_cross",
        jax.ShapeDtypeStruct(cq.shape, BF16), [VM] * (1 + count) + [ANY] * len(after), VM,
        (cq, *audios, *after), 8, flops=4 * count * (audios[0].shape[0] // 3) * cq.size,
    )


def merge_kernel(last, pieces, *refs):
    mine, came, outs = refs[:pieces], refs[pieces], refs[-pieces:]
    at = 0
    for one, out in zip(mine, outs):
        rows, end = one.shape[0], one.shape[1] - HD
        two = came.at[at : at + rows]
        at += rows
        levels = []
        for head in range(end // HD):
            columns = slice(head * HD, (head + 1) * HD)
            left, right = level_of(one[:, end:], head), level_of(two[:, end:], head)
            highest = jnp.maximum(left, right)
            left, right = jnp.exp2(left - highest), jnp.exp2(right - highest)
            mixed = one[:, columns].astype(F32) * left + two[:, columns].astype(F32) * right
            out[:, columns] = (mixed / (left + right)).astype(BF16)
            levels.append(highest + jnp.log2(left + right))
        if not last:
            out[:, end:] = stats_of(levels, rows)


def merge(mine, came, last, after=()):
    cut = HD if last else 0
    shapes = [jax.ShapeDtypeStruct((x.shape[0], x.shape[1] - cut), BF16) for x in mine]
    return call(
        functools.partial(merge_kernel, last, len(mine)), "merge_last" if last else "merge", shapes,
        [VM] * (len(mine) + 1) + [ANY] * len(after), [VM] * len(mine), (*mine, came, *after), 4,
    )


def exchanged(count, tensor, video_query, video_key, video_value, video_stream, out_weight,
              cross_query, audio_key, audio_value, audio_query, cross_key, cross_value):
    rows = video_query.shape[0]
    share = out_weight.shape[1] // tensor
    seq = [partner("seq", count, mask) for mask in range(count)]
    order = list(range(count - 1, 0, -1))
    audio_mask = 0

    packs = [None] * count
    sources = (video_query, video_key, video_value, audio_key, audio_value, audio_query)
    *made, own_audio = pack(order + [0], count, audio_mask, *sources)
    for mask, one in zip(order + [0], made):
        packs[mask] = one
    weight, cross_query, cross_key, cross_value, video_stream = fetch(
        out_weight, cross_query, cross_key, cross_value, video_stream
    )
    for mask in order:
        packs[mask] = seq[mask](packs[mask])
    audios = [own_audio if mask in (0, audio_mask) else seq[mask](own_audio) for mask in range(count)]
    if audio_mask:
        audios[audio_mask] = packs[audio_mask]
    heads = [None] * count
    for index, mask in enumerate(order + [0]):
        (heads[mask],) = attend([mask], order + [0], rows, packs, [weight], f"attend{index}")
    own_heads = list(heads)
    for mask in order:
        heads[mask] = seq[mask](heads[mask])

    groups = [(0, 1)] + [(1 << bit, 1 << bit) for bit in range(count.bit_length() - 1)]
    pieces = partials(
        groups, audio_mask, 3 * rows, cross_key, cross_value, audios, [own_heads[1]]
    )
    others = list(range(2, tensor, 2))
    core = partner("tensor", tensor, 1)
    sent = project(
        order + [0], heads, weight, share, {mask + 1: BF16 for mask in others}, "project_far",
        pieces[:1],
    )
    got = [core(x) for x in sent]
    pieces = list(pieces)
    kept = project(order + [0], heads, weight, share, {mask: F32 for mask in others}, "project_kept")
    summed = [(mine + theirs.astype(F32)).astype(BF16) for mine, theirs in zip(kept, got)]
    own, near = project(order + [0], heads, weight, share, {1: BF16, 0: F32}, "project_near", summed)
    total = video_stream.astype(F32) + near + core(own).astype(F32)
    for mask, piece in zip(others, summed):
        total = total + partner("tensor", tensor, mask)(piece).astype(F32)
    video_next = total.astype(BF16)
    video_cross = crossed(audio_mask, 3 * rows, cross_query, audios, summed)
    while len(pieces) > 2:
        mask = groups[len(pieces) - 1][0]
        came = seq[mask](pieces.pop())
        pieces = list(merge(pieces, came, False, summed))
    (audio_cross,) = merge(pieces[:1], seq[1](pieces[1]), True)
    return video_next, video_cross, audio_cross


def blank_state(query_rows, head_count):
    return (
        jnp.full((head_count, query_rows), -1e30, jnp.float32),
        jnp.zeros((head_count, query_rows), jnp.float32),
        jnp.zeros((head_count, query_rows, HD), jnp.float32),
    )


def absorb(carried, queries, keyset, values, head_count):
    running, row_sum, numerator = carried
    query_rows = queries.shape[0]
    key_rows = keyset.shape[0]
    factor = 1.0 / math.sqrt(HD)
    query_heads = queries.reshape(query_rows, head_count, HD)
    for offset in range(0, key_rows, 1024):
        width_keys = min(1024, key_rows - offset)
        key_block = keyset[offset : offset + width_keys].reshape(width_keys, head_count, HD)
        value_block = values[offset : offset + width_keys].reshape(width_keys, head_count, HD)
        scores = (
            jnp.einsum("qhd,khd->hqk", query_heads, key_block, preferred_element_type=jnp.float32)
            * factor
        )
        highest = jnp.maximum(running, jnp.max(scores, axis=2))
        raised = jnp.exp(scores - highest[:, :, None])
        shrink = jnp.exp(running - highest)
        row_sum = row_sum * shrink + jnp.sum(raised, axis=2)
        numerator = numerator * shrink[:, :, None] + jnp.einsum(
            "hqk,khd->hqd",
            raised.astype(jnp.bfloat16),
            value_block,
            preferred_element_type=jnp.float32,
        )
        running = highest
    return (running, row_sum, numerator)


def finish(carried, head_count):
    running, row_sum, numerator = carried
    result = numerator / row_sum[:, :, None]
    return result.transpose(1, 0, 2).reshape(result.shape[1], head_count * HD).astype(jnp.bfloat16)


def gathered(
    video_query,
    video_key,
    video_value,
    video_stream,
    out_weight,
    cross_query,
    audio_key,
    audio_value,
    audio_query,
    cross_key,
    cross_value,
):
    local_heads = video_query.shape[1] // HD
    query_rows = video_query.shape[0]
    pieces = (
        lax.all_gather(video_key, "seq", axis=0, tiled=True),
        lax.all_gather(video_value, "seq", axis=0, tiled=True),
    )
    carried_video = absorb(
        blank_state(query_rows, local_heads), video_query, pieces[0], pieces[1], local_heads
    )
    attended = finish(carried_video, local_heads)
    projected = jnp.dot(attended, out_weight, preferred_element_type=jnp.float32)
    summed = lax.psum_scatter(
        projected.astype(jnp.bfloat16), "tensor", scatter_dimension=1, tiled=True
    ).astype(jnp.float32)
    video_next = (video_stream.astype(jnp.float32) + summed).astype(jnp.bfloat16)
    cross_heads = cross_query.shape[1] // HD
    every_key, every_value = (
        lax.all_gather(audio_key, "seq", axis=0, tiled=True),
        lax.all_gather(audio_value, "seq", axis=0, tiled=True),
    )
    carried_audio = absorb(
        blank_state(cross_query.shape[0], cross_heads),
        cross_query,
        every_key,
        every_value,
        cross_heads,
    )
    video_cross = finish(carried_audio, cross_heads)
    pieces = (
        lax.all_gather(cross_key, "seq", axis=0, tiled=True),
        lax.all_gather(cross_value, "seq", axis=0, tiled=True),
    )
    carried_cross = absorb(
        blank_state(audio_query.shape[0], cross_heads),
        audio_query,
        pieces[0],
        pieces[1],
        cross_heads,
    )
    audio_cross = finish(carried_cross, cross_heads)
    return (video_next, video_cross, audio_cross)


def solution(mesh):
    count, tensor = mesh.shape["seq"], mesh.shape["tensor"]
    both = P(("groups", "seq"), "tensor")
    in_specs = (both,) * 4 + (P("tensor", None),) + (both,) * 6

    def local(*arrays):
        heads = arrays[0].shape[1] // HD
        powers = all(n > 1 and n & (n - 1) == 0 for n in (count, tensor))
        whole = heads % count == 0 and arrays[6].shape[0] % 16 == 0
        if powers and whole and arrays[6].shape[1] % (arrays[0].shape[1] // count) == 0:
            return exchanged(count, tensor, *arrays)
        return gathered(*arrays)

    return jax.shard_map(local, mesh=mesh, in_specs=in_specs, out_specs=(both,) * 3, check_vma=False)
```

```python
import functools
import math

import jax
import jax.numpy as jnp
from jax import lax
from jax.experimental import pallas as pl
from jax.experimental.pallas import tpu as pltpu
from jax.sharding import PartitionSpec as P


HD = 128
FACTOR = 1.0 / math.sqrt(HD)
LOG2E = math.log2(math.e)
BF16 = jnp.bfloat16
F32 = jnp.float32
MIB = 1 << 20
ANY = pl.BlockSpec(memory_space=pl.ANY)
HBM = pl.BlockSpec(memory_space=pltpu.HBM)
VM = pl.BlockSpec(memory_space=pltpu.VMEM)
WHOLE_VMEM = 62.75


COSTS = {"merge": 10000000000, "partials": 3000000000}


def call(kernel, name, shapes, ins, outs, operands, limit, scratch=(), flops=0):
    flops = COSTS.get(name, flops)
    return pl.pallas_call(
        kernel,
        out_shape=shapes,
        in_specs=ins,
        out_specs=outs,
        scratch_shapes=scratch,
        compiler_params=pltpu.CompilerParams(vmem_limit_bytes=int(limit * MIB)),
        cost_estimate=pl.CostEstimate(flops=flops, bytes_accessed=0, transcendentals=0),
        name=name,
    )(*operands)


def partner(axis, size, mask):
    return functools.partial(
        lax.ppermute, axis_name=axis, perm=[(i, i ^ mask) for i in range(size)]
    )


def nt(a, b):
    return lax.dot_general(a, b, (((1,), (1,)), ((), ())), preferred_element_type=F32)


def softmax_times(scores, value):
    highest = jnp.max(scores, axis=1, keepdims=True)
    raised = jnp.exp2(scores * (FACTOR * LOG2E) - highest * (FACTOR * LOG2E))
    total = jnp.sum(raised, axis=1, keepdims=True)
    numerator = jnp.dot(raised.astype(BF16), value, preferred_element_type=F32)
    return highest, total, numerator


def pack_kernel(masks, count, q, k, v, *rest):
    outs, sem = rest[:-1], rest[-1]
    rows, width = q.shape[0], q.shape[1] // count
    z = lax.axis_index("seq")
    copies = []
    for mask, out in zip(masks, outs):
        columns = pl.ds(pl.multiple_of(jnp.bitwise_xor(z, mask) * width, width), width)
        for position, source in enumerate((q, k, v)):
            target = out.at[pl.ds(position * rows, rows)]
            copies.append(pltpu.make_async_copy(source.at[:, columns], target, sem.at[len(copies)]))
            copies[-1].start()
    for one in copies:
        one.wait()


def pack(masks, count, q, k, v):
    shape = pltpu.VMEM((3 * q.shape[0], q.shape[1] // count), BF16)
    return call(
        functools.partial(pack_kernel, masks, count), "pack", [shape] * len(masks), [HBM] * 3, [VM] * len(masks),
        (q, k, v), WHOLE_VMEM, [pltpu.SemaphoreType.DMA((3 * len(masks),))],
    )


def attend_kernel(wanted, order, rows, *refs):
    count = len(order)
    packs, outs = dict(zip(order, refs)), refs[-len(wanted) :]
    for columns in range(0, packs[0].shape[1], HD):
        columns = slice(columns, columns + HD)
        key = jnp.concatenate([p[rows : 2 * rows, columns] for p in packs.values()], axis=0)
        value = jnp.concatenate([p[2 * rows : 3 * rows, columns] for p in packs.values()], axis=0)
        for mask, out in zip(wanted, outs):
            _, total, numerator = softmax_times(nt(packs[mask][:rows, columns], key), value)
            out[:, columns] = (numerator / total).astype(BF16)


def attend(wanted, order, rows, packs, after, name):
    count, width = len(packs), packs[0].shape[1]
    return call(
        functools.partial(attend_kernel, wanted, order, rows), name,
        [jax.ShapeDtypeStruct((rows, width), BF16)] * len(wanted),
        [VM] * count + [ANY] * len(after), [VM] * len(wanted), (*(packs[mask] for mask in order), *after), 8,
        flops=4 * count * len(wanted) * rows * rows * width,
    )


def fetch_kernel(count, *refs):
    pairs = list(zip(refs[:count], refs[count + 3 : 2 * count + 3]))
    own_audio, rows = refs[2 * count + 3], refs[count].shape[0]
    pairs += [(one, own_audio.at[pl.ds(kind * rows, rows)]) for kind, one in enumerate(refs[count : count + 3])]
    copies = [pltpu.make_async_copy(*pair, refs[-1].at[i]) for i, pair in enumerate(pairs)]
    for one in copies:
        one.start()
    for one in copies:
        one.wait()


def fetch(arrays, audio):
    count = len(arrays)
    shapes = [pltpu.VMEM(x.shape, x.dtype) for x in arrays]
    shapes.append(pltpu.VMEM((3 * audio[0].shape[0], audio[0].shape[1]), BF16))
    return call(
        functools.partial(fetch_kernel, count), "fetch", shapes, [HBM] * (count + 3), [VM] * (count + 1),
        (*arrays, *audio), 53, [pltpu.SemaphoreType.DMA((count + 3,))],
    )


def project_kernel(order, blocks, step, *refs):
    count = len(order)
    heads, w, lhs = refs[:count], refs[count], refs[-1]
    outs = refs[-1 - len(blocks) : -1]
    width = heads[0].shape[1]
    z = lax.axis_index("seq")
    t = lax.axis_index("tensor")
    for mask, one in zip(order, heads):
        owner = jnp.bitwise_xor(z, mask)
        lhs[:, pl.ds(pl.multiple_of(owner * width, width), width)] = one[...]
    for out, mask in zip(outs, blocks):
        share = out.shape[1]
        owner = jnp.bitwise_xor(t, mask)
        for start in range(0, share, step):
            columns = pl.ds(pl.multiple_of(owner * share + start, step), step)
            product = jnp.dot(lhs[...], w[:, columns], preferred_element_type=F32)
            out[:, start : start + step] = product.astype(out.dtype)


def project(order, heads, w, share, blocks, name, after=()):
    count, rows = len(heads), heads[0].shape[0]
    return call(
        functools.partial(project_kernel, order, list(blocks), math.gcd(512, share)), name,
        [jax.ShapeDtypeStruct((rows, share), dtype) for dtype in blocks.values()],
        [VM] * (count + 1) + [ANY] * len(after), [VM] * len(blocks), (*(heads[mask] for mask in order), w, *after), 8,
        [pltpu.VMEM((rows, w.shape[0]), BF16)],
        flops=2 * rows * w.shape[0] * share * len(blocks),
    )


def stats_of(levels, rows):
    lane = lax.broadcasted_iota(jnp.int32, (rows, HD), 1)
    stats = jnp.zeros((rows, HD), F32)
    for head, level in enumerate(levels):
        for piece in range(3):
            rounded = level.astype(BF16).astype(F32)
            stats = jnp.where(lane == 3 * head + piece, rounded, stats)
            level = level - rounded
    return stats.astype(BF16)


def level_of(stats, head):
    return jnp.sum(stats[:, 3 * head : 3 * head + 3].astype(F32), axis=1, keepdims=True)


def audio_of(audios, kind, head):
    rows = audios[0].shape[0] // 3
    here = (slice(kind * rows, (kind + 1) * rows), slice(head * HD, (head + 1) * HD))
    return jnp.concatenate([one[here] for one in audios], axis=0)


def partial_kernel(groups, ck, cv, *refs):
    count = sum(size for _, size in groups)
    audios, parts = refs[:count], refs[-len(groups) :]
    arows = audios[0].shape[0] // 3
    heads = ck.shape[1] // HD
    levels = []
    for head in range(heads):
        columns = slice(head * HD, (head + 1) * HD)
        highest, total, numerator = softmax_times(nt(audio_of(audios, 2, head), ck[:, columns]), cv[:, columns])
        partial = (numerator / total).astype(BF16)
        levels.append(highest * (FACTOR * LOG2E) + jnp.log2(total))
        for (start, size), part in zip(groups, parts):
            part[:, columns] = partial[start * arows : (start + size) * arows]
    stats = stats_of(levels, count * arows)
    for (start, size), part in zip(groups, parts):
        part[:, heads * HD :] = stats[start * arows : (start + size) * arows]


def partials(groups, ck, cv, audios, after):
    count = len(audios)
    arows = audios[0].shape[0] // 3
    return call(
        functools.partial(partial_kernel, groups), "partials",
        [jax.ShapeDtypeStruct((size * arows, ck.shape[1] + HD), BF16) for _, size in groups],
        [VM] * (2 + count) + [ANY] * len(after), [VM] * len(groups),
        (ck, cv, *audios, *after), 8, flops=4 * count * arows * ck.size,
    )


def video_cross_kernel(count, cq, *refs):
    audios, out = refs[:count], refs[-1]
    for head in range(cq.shape[1] // HD):
        columns = slice(head * HD, (head + 1) * HD)
        _, total, numerator = softmax_times(nt(cq[:, columns], audio_of(audios, 0, head)), audio_of(audios, 1, head))
        out[:, columns] = (numerator / total).astype(BF16)


def crossed(cq, audios, after):
    count = len(audios)
    return call(
        functools.partial(video_cross_kernel, count), "video_cross",
        jax.ShapeDtypeStruct(cq.shape, BF16), [VM] * (1 + count) + [ANY] * len(after), VM,
        (cq, *audios, *after), 8, flops=4 * count * (audios[0].shape[0] // 3) * cq.size,
    )


def merge_kernel(last, pieces, *refs):
    mine, came, outs = refs[:pieces], refs[pieces], refs[-pieces:]
    at = 0
    for one, out in zip(mine, outs):
        rows, end = one.shape[0], one.shape[1] - HD
        two = came.at[at : at + rows]
        at += rows
        levels = []
        for head in range(end // HD):
            columns = slice(head * HD, (head + 1) * HD)
            left, right = level_of(one[:, end:], head), level_of(two[:, end:], head)
            highest = jnp.maximum(left, right)
            left, right = jnp.exp2(left - highest), jnp.exp2(right - highest)
            mixed = one[:, columns].astype(F32) * left + two[:, columns].astype(F32) * right
            out[:, columns] = (mixed / (left + right)).astype(BF16)
            levels.append(highest + jnp.log2(left + right))
        if not last:
            out[:, end:] = stats_of(levels, rows)


def merge(mine, came, last, after=()):
    cut = HD if last else 0
    shapes = [jax.ShapeDtypeStruct((x.shape[0], x.shape[1] - cut), BF16) for x in mine]
    return call(
        functools.partial(merge_kernel, last, len(mine)), "merge_last" if last else "merge", shapes,
        [VM] * (len(mine) + 1) + [ANY] * len(after), [VM] * len(mine), (*mine, came, *after), 4,
    )


def exchanged(count, tensor, video_query, video_key, video_value, video_stream, out_weight,
              cross_query, audio_key, audio_value, audio_query, cross_key, cross_value):
    rows = video_query.shape[0]
    share = out_weight.shape[1] // tensor
    seq = [partner("seq", count, mask) for mask in range(count)]
    order = list(range(count - 1, 0, -1))

    packs = [None] * count
    for mask, one in zip(order + [0], pack(order + [0], count, video_query, video_key, video_value)):
        packs[mask] = one
    weight, cross_query, cross_key, cross_value, video_stream, own_audio = fetch(
        (out_weight, cross_query, cross_key, cross_value, video_stream), (audio_key, audio_value, audio_query)
    )
    for mask in order:
        packs[mask] = seq[mask](packs[mask])
    audios = [own_audio]
    for mask in range(1, count):
        if mask % 2 and mask > 1:
            audios.append(seq[1](audios[mask - 1]))
        else:
            audios.append(seq[mask](own_audio))
    heads = [None] * count
    for index, mask in enumerate(order + [0]):
        (heads[mask],) = attend([mask], order + [0], rows, packs, [weight], f"attend{index}")
    own_heads = list(heads)
    for mask in order:
        heads[mask] = seq[mask](heads[mask])

    groups = [(0, 1)] + [(1 << bit, 1 << bit) for bit in range(count.bit_length() - 1)]
    pieces = partials(
        groups, cross_key, cross_value, audios, [own_heads[1]]
    )
    others = list(range(2, tensor, 2))
    core = partner("tensor", tensor, 1)
    pieces = list(pieces)
    sent = project(order + [0], heads, weight, share, {mask + 1: BF16 for mask in others}, "project_far", pieces[:1])
    got = [core(x) for x in sent]
    kept = project(order + [0], heads, weight, share, {mask: F32 for mask in others}, "project_kept", sent[:1])
    summed = [(mine + theirs.astype(F32)).astype(BF16) for mine, theirs in zip(kept, got)]
    own, near = project(order + [0], heads, weight, share, {1: BF16, 0: F32}, "project_near", summed)
    total = video_stream.astype(F32) + near + core(own).astype(F32)
    for mask, piece in zip(others, summed):
        total = total + partner("tensor", tensor, mask)(piece).astype(F32)
    video_next = total.astype(BF16)
    video_cross = crossed(cross_query, audios, summed)
    while len(pieces) > 2:
        mask = groups[len(pieces) - 1][0]
        other = seq[mask](pieces.pop())
        pieces = list(merge(pieces, other, False, summed))
    (audio_cross,) = merge(pieces[:1], seq[1](pieces[1]), True)
    return video_next, video_cross, audio_cross


def blank_state(query_rows, head_count):
    return (
        jnp.full((head_count, query_rows), -1e30, jnp.float32),
        jnp.zeros((head_count, query_rows), jnp.float32),
        jnp.zeros((head_count, query_rows, HD), jnp.float32),
    )


def absorb(carried, queries, keyset, values, head_count):
    running, row_sum, numerator = carried
    query_rows = queries.shape[0]
    key_rows = keyset.shape[0]
    factor = 1.0 / math.sqrt(HD)
    query_heads = queries.reshape(query_rows, head_count, HD)
    for offset in range(0, key_rows, 1024):
        width_keys = min(1024, key_rows - offset)
        key_block = keyset[offset : offset + width_keys].reshape(width_keys, head_count, HD)
        value_block = values[offset : offset + width_keys].reshape(width_keys, head_count, HD)
        scores = (
            jnp.einsum("qhd,khd->hqk", query_heads, key_block, preferred_element_type=jnp.float32)
            * factor
        )
        highest = jnp.maximum(running, jnp.max(scores, axis=2))
        raised = jnp.exp(scores - highest[:, :, None])
        shrink = jnp.exp(running - highest)
        row_sum = row_sum * shrink + jnp.sum(raised, axis=2)
        numerator = numerator * shrink[:, :, None] + jnp.einsum(
            "hqk,khd->hqd",
            raised.astype(jnp.bfloat16),
            value_block,
            preferred_element_type=jnp.float32,
        )
        running = highest
    return (running, row_sum, numerator)


def finish(carried, head_count):
    running, row_sum, numerator = carried
    result = numerator / row_sum[:, :, None]
    return result.transpose(1, 0, 2).reshape(result.shape[1], head_count * HD).astype(jnp.bfloat16)


def gathered(
    video_query,
    video_key,
    video_value,
    video_stream,
    out_weight,
    cross_query,
    audio_key,
    audio_value,
    audio_query,
    cross_key,
    cross_value,
):
    local_heads = video_query.shape[1] // HD
    query_rows = video_query.shape[0]
    pieces = (
        lax.all_gather(video_key, "seq", axis=0, tiled=True),
        lax.all_gather(video_value, "seq", axis=0, tiled=True),
    )
    carried_video = absorb(
        blank_state(query_rows, local_heads), video_query, pieces[0], pieces[1], local_heads
    )
    attended = finish(carried_video, local_heads)
    projected = jnp.dot(attended, out_weight, preferred_element_type=jnp.float32)
    summed = lax.psum_scatter(
        projected.astype(jnp.bfloat16), "tensor", scatter_dimension=1, tiled=True
    ).astype(jnp.float32)
    video_next = (video_stream.astype(jnp.float32) + summed).astype(jnp.bfloat16)
    cross_heads = cross_query.shape[1] // HD
    every_key, every_value = (
        lax.all_gather(audio_key, "seq", axis=0, tiled=True),
        lax.all_gather(audio_value, "seq", axis=0, tiled=True),
    )
    carried_audio = absorb(
        blank_state(cross_query.shape[0], cross_heads),
        cross_query,
        every_key,
        every_value,
        cross_heads,
    )
    video_cross = finish(carried_audio, cross_heads)
    pieces = (
        lax.all_gather(cross_key, "seq", axis=0, tiled=True),
        lax.all_gather(cross_value, "seq", axis=0, tiled=True),
    )
    carried_cross = absorb(
        blank_state(audio_query.shape[0], cross_heads),
        audio_query,
        pieces[0],
        pieces[1],
        cross_heads,
    )
    audio_cross = finish(carried_cross, cross_heads)
    return (video_next, video_cross, audio_cross)


def solution(mesh):
    count, tensor = mesh.shape["seq"], mesh.shape["tensor"]
    both = P(("groups", "seq"), "tensor")
    in_specs = (both,) * 4 + (P("tensor", None),) + (both,) * 6

    def local(*arrays):
        heads = arrays[0].shape[1] // HD
        powers = all(n > 1 and n & (n - 1) == 0 for n in (count, tensor))
        if powers and heads % count == 0 and arrays[6].shape[0] % 16 == 0:
            return exchanged(count, tensor, *arrays)
        return gathered(*arrays)

    return jax.shard_map(local, mesh=mesh, in_specs=in_specs, out_specs=(both,) * 3, check_vma=False)
```

```python
import functools
import math

import jax
import jax.numpy as jnp
from jax import lax
from jax.experimental import pallas as pl
from jax.experimental.pallas import tpu as pltpu
from jax.sharding import PartitionSpec as P


HD = 128
FACTOR = 1.0 / math.sqrt(HD)
LOG2E = math.log2(math.e)
BF16 = jnp.bfloat16
F32 = jnp.float32
MIB = 1 << 20
ANY = pl.BlockSpec(memory_space=pl.ANY)
HBM = pl.BlockSpec(memory_space=pltpu.HBM)
VM = pl.BlockSpec(memory_space=pltpu.VMEM)
WHOLE_VMEM = 62.75


COSTS = {"merge": 10000000000, "partials": 3000000000, "project_kept": 10000000000}


def call(kernel, name, shapes, ins, outs, operands, limit, scratch=(), flops=0):
    flops = COSTS.get(name, flops)
    return pl.pallas_call(
        kernel,
        out_shape=shapes,
        in_specs=ins,
        out_specs=outs,
        scratch_shapes=scratch,
        compiler_params=pltpu.CompilerParams(vmem_limit_bytes=int(limit * MIB)),
        cost_estimate=pl.CostEstimate(flops=flops, bytes_accessed=0, transcendentals=0),
        name=name,
    )(*operands)


def partner(axis, size, mask):
    return functools.partial(
        lax.ppermute, axis_name=axis, perm=[(i, i ^ mask) for i in range(size)]
    )


def nt(a, b):
    return lax.dot_general(a, b, (((1,), (1,)), ((), ())), preferred_element_type=F32)


def softmax_times(scores, value):
    highest = jnp.max(scores, axis=1, keepdims=True)
    raised = jnp.exp2(scores * (FACTOR * LOG2E) - highest * (FACTOR * LOG2E))
    total = jnp.sum(raised, axis=1, keepdims=True)
    numerator = jnp.dot(raised.astype(BF16), value, preferred_element_type=F32)
    return highest, total, numerator


def pack_kernel(masks, count, q, k, v, *rest):
    outs, sem = rest[:-1], rest[-1]
    rows, width = q.shape[0], q.shape[1] // count
    z = lax.axis_index("seq")
    copies = []
    for mask, out in zip(masks, outs):
        columns = pl.ds(pl.multiple_of(jnp.bitwise_xor(z, mask) * width, width), width)
        for position, source in enumerate((q, k, v)):
            target = out.at[pl.ds(position * rows, rows)]
            copies.append(pltpu.make_async_copy(source.at[:, columns], target, sem.at[len(copies)]))
            copies[-1].start()
    for one in copies:
        one.wait()


def pack(masks, count, q, k, v):
    shape = pltpu.VMEM((3 * q.shape[0], q.shape[1] // count), BF16)
    return call(
        functools.partial(pack_kernel, masks, count), "pack", [shape] * len(masks), [HBM] * 3, [VM] * len(masks),
        (q, k, v), WHOLE_VMEM, [pltpu.SemaphoreType.DMA((3 * len(masks),))],
    )


def attend_kernel(wanted, order, rows, *refs):
    count = len(order)
    packs, outs = dict(zip(order, refs)), refs[-len(wanted) :]
    for columns in range(0, packs[0].shape[1], HD):
        columns = slice(columns, columns + HD)
        key = jnp.concatenate([p[rows : 2 * rows, columns] for p in packs.values()], axis=0)
        value = jnp.concatenate([p[2 * rows : 3 * rows, columns] for p in packs.values()], axis=0)
        for mask, out in zip(wanted, outs):
            _, total, numerator = softmax_times(nt(packs[mask][:rows, columns], key), value)
            out[:, columns] = (numerator / total).astype(BF16)


def attend(wanted, order, rows, packs, after, name):
    count, width = len(packs), packs[0].shape[1]
    return call(
        functools.partial(attend_kernel, wanted, order, rows), name,
        [jax.ShapeDtypeStruct((rows, width), BF16)] * len(wanted),
        [VM] * count + [ANY] * len(after), [VM] * len(wanted), (*(packs[mask] for mask in order), *after), 8,
        flops=4 * count * len(wanted) * rows * rows * width,
    )


def fetch_kernel(count, *refs):
    pairs = list(zip(refs[:count], refs[count + 3 : 2 * count + 3]))
    own_audio, rows = refs[2 * count + 3], refs[count].shape[0]
    pairs += [(one, own_audio.at[pl.ds(kind * rows, rows)]) for kind, one in enumerate(refs[count : count + 3])]
    copies = [pltpu.make_async_copy(*pair, refs[-1].at[i]) for i, pair in enumerate(pairs)]
    for one in copies:
        one.start()
    for one in copies:
        one.wait()


def fetch(arrays, audio):
    count = len(arrays)
    shapes = [pltpu.VMEM(x.shape, x.dtype) for x in arrays]
    shapes.append(pltpu.VMEM((3 * audio[0].shape[0], audio[0].shape[1]), BF16))
    return call(
        functools.partial(fetch_kernel, count), "fetch", shapes, [HBM] * (count + 3), [VM] * (count + 1),
        (*arrays, *audio), 53, [pltpu.SemaphoreType.DMA((count + 3,))],
    )


def project_kernel(order, blocks, part, step, *refs):
    count = len(order)
    heads, w, lhs = refs[:count], refs[count], refs[-1]
    outs = refs[-1 - len(blocks) : -1]
    width = heads[0].shape[1]
    z = lax.axis_index("seq")
    t = lax.axis_index("tensor")
    for mask, one in zip(order, heads):
        owner = jnp.bitwise_xor(z, mask)
        lhs[:, pl.ds(pl.multiple_of(owner * width, width), width)] = one[...]
    part, parts = part
    for out, mask in zip(outs, blocks):
        share = out.shape[1]
        owner = jnp.bitwise_xor(t, mask)
        for start in range(0, share, step):
            columns = pl.ds(pl.multiple_of((owner * parts + part) * share + start, step), step)
            product = jnp.dot(lhs[...], w[:, columns], preferred_element_type=F32)
            out[:, start : start + step] = product.astype(out.dtype)


def project(order, heads, w, share, blocks, name, after=(), part=(0, 1)):
    count, rows = len(heads), heads[0].shape[0]
    return call(
        functools.partial(project_kernel, order, list(blocks), part, math.gcd(512, share)), name,
        [jax.ShapeDtypeStruct((rows, share), dtype) for dtype in blocks.values()],
        [VM] * (count + 1) + [ANY] * len(after), [VM] * len(blocks), (*(heads[mask] for mask in order), w, *after), 8,
        [pltpu.VMEM((rows, w.shape[0]), BF16)],
        flops=2 * rows * w.shape[0] * share * len(blocks),
    )


def stats_of(levels, rows):
    lane = lax.broadcasted_iota(jnp.int32, (rows, HD), 1)
    stats = jnp.zeros((rows, HD), F32)
    for head, level in enumerate(levels):
        for piece in range(3):
            rounded = level.astype(BF16).astype(F32)
            stats = jnp.where(lane == 3 * head + piece, rounded, stats)
            level = level - rounded
    return stats.astype(BF16)


def level_of(stats, head):
    return jnp.sum(stats[:, 3 * head : 3 * head + 3].astype(F32), axis=1, keepdims=True)


def audio_of(audios, kind, head):
    rows = audios[0].shape[0] // 3
    here = (slice(kind * rows, (kind + 1) * rows), slice(head * HD, (head + 1) * HD))
    return jnp.concatenate([one[here] for one in audios], axis=0)


def partial_kernel(groups, ck, cv, *refs):
    count = sum(size for _, size in groups)
    audios, parts = refs[:count], refs[-len(groups) :]
    arows = audios[0].shape[0] // 3
    heads = ck.shape[1] // HD
    levels = []
    for head in range(heads):
        columns = slice(head * HD, (head + 1) * HD)
        highest, total, numerator = softmax_times(nt(audio_of(audios, 2, head), ck[:, columns]), cv[:, columns])
        partial = (numerator / total).astype(BF16)
        levels.append(highest * (FACTOR * LOG2E) + jnp.log2(total))
        for (start, size), part in zip(groups, parts):
            part[:, columns] = partial[start * arows : (start + size) * arows]
    stats = stats_of(levels, count * arows)
    for (start, size), part in zip(groups, parts):
        part[:, heads * HD :] = stats[start * arows : (start + size) * arows]


def partials(groups, ck, cv, audios, after):
    count = len(audios)
    arows = audios[0].shape[0] // 3
    return call(
        functools.partial(partial_kernel, groups), "partials",
        [jax.ShapeDtypeStruct((size * arows, ck.shape[1] + HD), BF16) for _, size in groups],
        [VM] * (2 + count) + [ANY] * len(after), [VM] * len(groups),
        (ck, cv, *audios, *after), 8, flops=4 * count * arows * ck.size,
    )


def video_cross_kernel(count, cq, *refs):
    audios, out = refs[:count], refs[-1]
    for head in range(cq.shape[1] // HD):
        columns = slice(head * HD, (head + 1) * HD)
        _, total, numerator = softmax_times(nt(cq[:, columns], audio_of(audios, 0, head)), audio_of(audios, 1, head))
        out[:, columns] = (numerator / total).astype(BF16)


def crossed(cq, audios, after):
    count = len(audios)
    return call(
        functools.partial(video_cross_kernel, count), "video_cross",
        jax.ShapeDtypeStruct(cq.shape, BF16), [VM] * (1 + count) + [ANY] * len(after), VM,
        (cq, *audios, *after), 8, flops=4 * count * (audios[0].shape[0] // 3) * cq.size,
    )


def merge_kernel(last, pieces, *refs):
    mine, came, outs = refs[:pieces], refs[pieces], refs[-pieces:]
    at = 0
    for one, out in zip(mine, outs):
        rows, end = one.shape[0], one.shape[1] - HD
        two = came.at[at : at + rows]
        at += rows
        levels = []
        for head in range(end // HD):
            columns = slice(head * HD, (head + 1) * HD)
            left, right = level_of(one[:, end:], head), level_of(two[:, end:], head)
            highest = jnp.maximum(left, right)
            left, right = jnp.exp2(left - highest), jnp.exp2(right - highest)
            mixed = one[:, columns].astype(F32) * left + two[:, columns].astype(F32) * right
            out[:, columns] = (mixed / (left + right)).astype(BF16)
            levels.append(highest + jnp.log2(left + right))
        if not last:
            out[:, end:] = stats_of(levels, rows)


def merge(mine, came, last, after=()):
    cut = HD if last else 0
    shapes = [jax.ShapeDtypeStruct((x.shape[0], x.shape[1] - cut), BF16) for x in mine]
    return call(
        functools.partial(merge_kernel, last, len(mine)), "merge_last" if last else "merge", shapes,
        [VM] * (len(mine) + 1) + [ANY] * len(after), [VM] * len(mine), (*mine, came, *after), 4,
    )


def exchanged(count, tensor, video_query, video_key, video_value, video_stream, out_weight,
              cross_query, audio_key, audio_value, audio_query, cross_key, cross_value):
    rows = video_query.shape[0]
    share = out_weight.shape[1] // tensor
    seq = [partner("seq", count, mask) for mask in range(count)]
    order = list(range(count - 1, 0, -1))

    packs = [None] * count
    for mask, one in zip(order + [0], pack(order + [0], count, video_query, video_key, video_value)):
        packs[mask] = one
    weight, cross_query, cross_key, cross_value, video_stream, own_audio = fetch(
        (out_weight, cross_query, cross_key, cross_value, video_stream), (audio_key, audio_value, audio_query)
    )
    for mask in order:
        packs[mask] = seq[mask](packs[mask])
    audios = [own_audio]
    for mask in range(1, count):
        if mask % 2 and mask > 1:
            audios.append(seq[1](audios[mask - 1]))
        else:
            audios.append(seq[mask](own_audio))
    heads = [None] * count
    done = [weight]
    for index, mask in enumerate(order + [0]):
        (heads[mask],) = attend([mask], order + [0], rows, packs, done, f"attend{index}")
        if mask:
            done = [heads[mask]]
    own_heads = list(heads)
    for mask in order:
        heads[mask] = seq[mask](heads[mask])

    groups = [(0, 1)] + [(1 << bit, 1 << bit) for bit in range(count.bit_length() - 1)]
    pieces = partials(
        groups, cross_key, cross_value, audios, [own_heads[1]]
    )
    others = list(range(2, tensor, 2))
    core = partner("tensor", tensor, 1)
    def halve(pieces, after):
        while len(pieces) > 2:
            mask = groups[len(pieces) - 1][0]
            other = seq[mask](pieces.pop())
            pieces = list(merge(pieces, other, False, after))
        return pieces

    pieces = list(pieces)
    chunks = 2 if share % 256 == 0 else 1
    got, after = [], pieces[:1]
    for part in range(chunks):
        sent = project(
            order + [0], heads, weight, share // chunks, {mask + 1: BF16 for mask in others}, "project_far", after,
            (part, chunks),
        )
        after = sent[:1]
        got.append([core(x) for x in sent])
    came = []
    for part in range(chunks):
        kept = project(
            order + [0], heads, weight, share // chunks, {mask: F32 for mask in others}, "project_kept", after,
            (part, chunks),
        )
        summed = [(mine + theirs.astype(F32)).astype(BF16) for mine, theirs in zip(kept, got[part])]
        came.append([partner("tensor", tensor, mask)(piece).astype(F32) for mask, piece in zip(others, summed)])
        after = summed[:1]
    own, near = project(order + [0], heads, weight, share, {1: BF16, 0: F32}, "project_near", summed)
    total = video_stream.astype(F32) + near + core(own).astype(F32)
    for index in range(len(others)):
        total = total + jnp.concatenate([one[index] for one in came], axis=1)
    video_next = total.astype(BF16)
    video_cross = crossed(cross_query, audios, summed)
    pieces = halve(pieces, summed)
    (audio_cross,) = merge(pieces[:1], seq[1](pieces[1]), True)
    return video_next, video_cross, audio_cross


def blank_state(query_rows, head_count):
    return (
        jnp.full((head_count, query_rows), -1e30, jnp.float32),
        jnp.zeros((head_count, query_rows), jnp.float32),
        jnp.zeros((head_count, query_rows, HD), jnp.float32),
    )


def absorb(carried, queries, keyset, values, head_count):
    running, row_sum, numerator = carried
    query_rows = queries.shape[0]
    key_rows = keyset.shape[0]
    factor = 1.0 / math.sqrt(HD)
    query_heads = queries.reshape(query_rows, head_count, HD)
    for offset in range(0, key_rows, 1024):
        width_keys = min(1024, key_rows - offset)
        key_block = keyset[offset : offset + width_keys].reshape(width_keys, head_count, HD)
        value_block = values[offset : offset + width_keys].reshape(width_keys, head_count, HD)
        scores = (
            jnp.einsum("qhd,khd->hqk", query_heads, key_block, preferred_element_type=jnp.float32)
            * factor
        )
        highest = jnp.maximum(running, jnp.max(scores, axis=2))
        raised = jnp.exp(scores - highest[:, :, None])
        shrink = jnp.exp(running - highest)
        row_sum = row_sum * shrink + jnp.sum(raised, axis=2)
        numerator = numerator * shrink[:, :, None] + jnp.einsum(
            "hqk,khd->hqd",
            raised.astype(jnp.bfloat16),
            value_block,
            preferred_element_type=jnp.float32,
        )
        running = highest
    return (running, row_sum, numerator)


def finish(carried, head_count):
    running, row_sum, numerator = carried
    result = numerator / row_sum[:, :, None]
    return result.transpose(1, 0, 2).reshape(result.shape[1], head_count * HD).astype(jnp.bfloat16)


def gathered(
    video_query,
    video_key,
    video_value,
    video_stream,
    out_weight,
    cross_query,
    audio_key,
    audio_value,
    audio_query,
    cross_key,
    cross_value,
):
    local_heads = video_query.shape[1] // HD
    query_rows = video_query.shape[0]
    pieces = (
        lax.all_gather(video_key, "seq", axis=0, tiled=True),
        lax.all_gather(video_value, "seq", axis=0, tiled=True),
    )
    carried_video = absorb(
        blank_state(query_rows, local_heads), video_query, pieces[0], pieces[1], local_heads
    )
    attended = finish(carried_video, local_heads)
    projected = jnp.dot(attended, out_weight, preferred_element_type=jnp.float32)
    summed = lax.psum_scatter(
        projected.astype(jnp.bfloat16), "tensor", scatter_dimension=1, tiled=True
    ).astype(jnp.float32)
    video_next = (video_stream.astype(jnp.float32) + summed).astype(jnp.bfloat16)
    cross_heads = cross_query.shape[1] // HD
    every_key, every_value = (
        lax.all_gather(audio_key, "seq", axis=0, tiled=True),
        lax.all_gather(audio_value, "seq", axis=0, tiled=True),
    )
    carried_audio = absorb(
        blank_state(cross_query.shape[0], cross_heads),
        cross_query,
        every_key,
        every_value,
        cross_heads,
    )
    video_cross = finish(carried_audio, cross_heads)
    pieces = (
        lax.all_gather(cross_key, "seq", axis=0, tiled=True),
        lax.all_gather(cross_value, "seq", axis=0, tiled=True),
    )
    carried_cross = absorb(
        blank_state(audio_query.shape[0], cross_heads),
        audio_query,
        pieces[0],
        pieces[1],
        cross_heads,
    )
    audio_cross = finish(carried_cross, cross_heads)
    return (video_next, video_cross, audio_cross)


def solution(mesh):
    count, tensor = mesh.shape["seq"], mesh.shape["tensor"]
    both = P(("groups", "seq"), "tensor")
    in_specs = (both,) * 4 + (P("tensor", None),) + (both,) * 6

    def local(*arrays):
        heads = arrays[0].shape[1] // HD
        powers = all(n > 1 and n & (n - 1) == 0 for n in (count, tensor))
        if powers and heads % count == 0 and arrays[6].shape[0] % 16 == 0:
            return exchanged(count, tensor, *arrays)
        return gathered(*arrays)

    return jax.shard_map(local, mesh=mesh, in_specs=in_specs, out_specs=(both,) * 3, check_vma=False)
```

```python
import functools
import math

import jax
import jax.numpy as jnp
from jax import lax
from jax.experimental import pallas as pl
from jax.experimental.pallas import tpu as pltpu
from jax.sharding import PartitionSpec as P


HD = 128
FACTOR = 1.0 / math.sqrt(HD)
LOG2E = math.log2(math.e)
BF16 = jnp.bfloat16
F32 = jnp.float32
MIB = 1 << 20
ANY = pl.BlockSpec(memory_space=pl.ANY)
HBM = pl.BlockSpec(memory_space=pltpu.HBM)
VM = pl.BlockSpec(memory_space=pltpu.VMEM)
WHOLE_VMEM = 62.75


COSTS = {"merge": 10000000000, "partials": 3000000000, "project_kept": 10000000000}


def call(kernel, name, shapes, ins, outs, operands, limit, scratch=(), flops=0):
    flops = COSTS.get(name, flops)
    return pl.pallas_call(
        kernel,
        out_shape=shapes,
        in_specs=ins,
        out_specs=outs,
        scratch_shapes=scratch,
        compiler_params=pltpu.CompilerParams(vmem_limit_bytes=int(limit * MIB)),
        cost_estimate=pl.CostEstimate(flops=flops, bytes_accessed=0, transcendentals=0),
        name=name,
    )(*operands)


def partner(axis, size, mask):
    return functools.partial(
        lax.ppermute, axis_name=axis, perm=[(i, i ^ mask) for i in range(size)]
    )


def nt(a, b):
    return lax.dot_general(a, b, (((1,), (1,)), ((), ())), preferred_element_type=F32)


def softmax_times(scores, value):
    highest = jnp.max(scores, axis=1, keepdims=True)
    raised = jnp.exp2(scores * (FACTOR * LOG2E) - highest * (FACTOR * LOG2E))
    total = jnp.sum(raised, axis=1, keepdims=True)
    numerator = jnp.dot(raised.astype(BF16), value, preferred_element_type=F32)
    return highest, total, numerator


def pack_kernel(masks, count, q, k, v, *rest):
    outs, sem = rest[:-1], rest[-1]
    rows, width = q.shape[0], q.shape[1] // count
    z = lax.axis_index("seq")
    copies = []
    for mask, out in zip(masks, outs):
        columns = pl.ds(pl.multiple_of(jnp.bitwise_xor(z, mask) * width, width), width)
        for position, source in enumerate((q, k, v)):
            target = out.at[pl.ds(position * rows, rows)]
            copies.append(pltpu.make_async_copy(source.at[:, columns], target, sem.at[len(copies)]))
            copies[-1].start()
    for one in copies:
        one.wait()


def pack(masks, count, q, k, v):
    shape = pltpu.VMEM((3 * q.shape[0], q.shape[1] // count), BF16)
    return call(
        functools.partial(pack_kernel, masks, count), "pack", [shape] * len(masks), [HBM] * 3, [VM] * len(masks),
        (q, k, v), WHOLE_VMEM, [pltpu.SemaphoreType.DMA((3 * len(masks),))],
    )


def attend_kernel(wanted, order, rows, carried, *refs):
    count = len(order)
    packs, outs = dict(zip(order, refs)), refs[-len(wanted) - carried :]
    for index in range(carried):
        refs[index - carried][...] = refs[count + index][...]
    for columns in range(0, packs[0].shape[1], HD):
        columns = slice(columns, columns + HD)
        key = jnp.concatenate([p[rows : 2 * rows, columns] for p in packs.values()], axis=0)
        value = jnp.concatenate([p[2 * rows : 3 * rows, columns] for p in packs.values()], axis=0)
        for mask, out in zip(wanted, outs):
            _, total, numerator = softmax_times(nt(packs[mask][:rows, columns], key), value)
            out[:, columns] = (numerator / total).astype(BF16)


def attend(wanted, order, rows, packs, after, name, carry=()):
    count, width = len(packs), packs[0].shape[1]
    return call(
        functools.partial(attend_kernel, wanted, order, rows, len(carry)), name,
        [jax.ShapeDtypeStruct((rows, width), BF16)] * len(wanted) + [jax.ShapeDtypeStruct(x.shape, x.dtype) for x in carry],
        [VM] * (count + len(carry)) + [ANY] * len(after), [VM] * (len(wanted) + len(carry)),
        (*(packs[mask] for mask in order), *carry, *after), 8,
        flops=4 * count * len(wanted) * rows * rows * width,
    )


def fetch_kernel(count, *refs):
    pairs = list(zip(refs[:count], refs[count + 3 : 2 * count + 3]))
    own_audio, rows = refs[2 * count + 3], refs[count].shape[0]
    pairs += [(one, own_audio.at[pl.ds(kind * rows, rows)]) for kind, one in enumerate(refs[count : count + 3])]
    copies = [pltpu.make_async_copy(*pair, refs[-1].at[i]) for i, pair in enumerate(pairs)]
    for one in copies:
        one.start()
    for one in copies:
        one.wait()


def fetch(arrays, audio):
    count = len(arrays)
    shapes = [pltpu.VMEM(x.shape, x.dtype) for x in arrays]
    shapes.append(pltpu.VMEM((3 * audio[0].shape[0], audio[0].shape[1]), BF16))
    return call(
        functools.partial(fetch_kernel, count), "fetch", shapes, [HBM] * (count + 3), [VM] * (count + 1),
        (*arrays, *audio), 53, [pltpu.SemaphoreType.DMA((count + 3,))],
    )


def project_kernel(order, blocks, part, step, *refs):
    count = len(order)
    heads, w, lhs = refs[:count], refs[count], refs[-1]
    outs = refs[-1 - len(blocks) : -1]
    width = heads[0].shape[1]
    z = lax.axis_index("seq")
    t = lax.axis_index("tensor")
    for mask, one in zip(order, heads):
        owner = jnp.bitwise_xor(z, mask)
        lhs[:, pl.ds(pl.multiple_of(owner * width, width), width)] = one[...]
    part, parts = part
    for out, mask in zip(outs, blocks):
        share = out.shape[1]
        owner = jnp.bitwise_xor(t, mask)
        for start in range(0, share, step):
            columns = pl.ds(pl.multiple_of((owner * parts + part) * share + start, step), step)
            product = jnp.dot(lhs[...], w[:, columns], preferred_element_type=F32)
            out[:, start : start + step] = product.astype(out.dtype)


def project(order, heads, w, share, blocks, name, after=(), part=(0, 1)):
    count, rows = len(heads), heads[0].shape[0]
    return call(
        functools.partial(project_kernel, order, list(blocks), part, math.gcd(512, share)), name,
        [jax.ShapeDtypeStruct((rows, share), dtype) for dtype in blocks.values()],
        [VM] * (count + 1) + [ANY] * len(after), [VM] * len(blocks), (*(heads[mask] for mask in order), w, *after), 8,
        [pltpu.VMEM((rows, w.shape[0]), BF16)],
        flops=2 * rows * w.shape[0] * share * len(blocks),
    )


def stats_of(levels, rows):
    lane = lax.broadcasted_iota(jnp.int32, (rows, HD), 1)
    stats = jnp.zeros((rows, HD), F32)
    for head, level in enumerate(levels):
        for piece in range(3):
            rounded = level.astype(BF16).astype(F32)
            stats = jnp.where(lane == 3 * head + piece, rounded, stats)
            level = level - rounded
    return stats.astype(BF16)


def level_of(stats, head):
    return jnp.sum(stats[:, 3 * head : 3 * head + 3].astype(F32), axis=1, keepdims=True)


def audio_of(audios, kind, head):
    rows = audios[0].shape[0] // 3
    here = (slice(kind * rows, (kind + 1) * rows), slice(head * HD, (head + 1) * HD))
    return jnp.concatenate([one[here] for one in audios], axis=0)


def partial_kernel(groups, ck, cv, *refs):
    count = sum(size for _, size in groups)
    audios, parts = refs[:count], refs[-len(groups) :]
    arows = audios[0].shape[0] // 3
    heads = ck.shape[1] // HD
    levels = []
    for head in range(heads):
        columns = slice(head * HD, (head + 1) * HD)
        highest, total, numerator = softmax_times(nt(audio_of(audios, 2, head), ck[:, columns]), cv[:, columns])
        partial = (numerator / total).astype(BF16)
        levels.append(highest * (FACTOR * LOG2E) + jnp.log2(total))
        for (start, size), part in zip(groups, parts):
            part[:, columns] = partial[start * arows : (start + size) * arows]
    stats = stats_of(levels, count * arows)
    for (start, size), part in zip(groups, parts):
        part[:, heads * HD :] = stats[start * arows : (start + size) * arows]


def partials(groups, ck, cv, audios, after):
    count = len(audios)
    arows = audios[0].shape[0] // 3
    return call(
        functools.partial(partial_kernel, groups), "partials",
        [jax.ShapeDtypeStruct((size * arows, ck.shape[1] + HD), BF16) for _, size in groups],
        [VM] * (2 + count) + [ANY] * len(after), [VM] * len(groups),
        (ck, cv, *audios, *after), 8, flops=4 * count * arows * ck.size,
    )


def video_cross_kernel(count, cq, *refs):
    audios, out = refs[:count], refs[-1]
    for head in range(cq.shape[1] // HD):
        columns = slice(head * HD, (head + 1) * HD)
        _, total, numerator = softmax_times(nt(cq[:, columns], audio_of(audios, 0, head)), audio_of(audios, 1, head))
        out[:, columns] = (numerator / total).astype(BF16)


def crossed(cq, audios, after):
    count = len(audios)
    return call(
        functools.partial(video_cross_kernel, count), "video_cross",
        jax.ShapeDtypeStruct(cq.shape, BF16), [VM] * (1 + count) + [ANY] * len(after), VM,
        (cq, *audios, *after), 8, flops=4 * count * (audios[0].shape[0] // 3) * cq.size,
    )


def merge_kernel(last, pieces, *refs):
    mine, came, outs = refs[:pieces], refs[pieces], refs[-pieces:]
    at = 0
    for one, out in zip(mine, outs):
        rows, end = one.shape[0], one.shape[1] - HD
        two = came.at[at : at + rows]
        at += rows
        levels = []
        for head in range(end // HD):
            columns = slice(head * HD, (head + 1) * HD)
            left, right = level_of(one[:, end:], head), level_of(two[:, end:], head)
            highest = jnp.maximum(left, right)
            left, right = jnp.exp2(left - highest), jnp.exp2(right - highest)
            mixed = one[:, columns].astype(F32) * left + two[:, columns].astype(F32) * right
            out[:, columns] = (mixed / (left + right)).astype(BF16)
            levels.append(highest + jnp.log2(left + right))
        if not last:
            out[:, end:] = stats_of(levels, rows)


def merge(mine, came, last, after=()):
    cut = HD if last else 0
    shapes = [jax.ShapeDtypeStruct((x.shape[0], x.shape[1] - cut), BF16) for x in mine]
    return call(
        functools.partial(merge_kernel, last, len(mine)), "merge_last" if last else "merge", shapes,
        [VM] * (len(mine) + 1) + [ANY] * len(after), [VM] * len(mine), (*mine, came, *after), 4,
    )


def exchanged(count, tensor, video_query, video_key, video_value, video_stream, out_weight,
              cross_query, audio_key, audio_value, audio_query, cross_key, cross_value):
    rows = video_query.shape[0]
    share = out_weight.shape[1] // tensor
    seq = [partner("seq", count, mask) for mask in range(count)]
    order = list(range(count - 1, 0, -1))

    packs = [None] * count
    for mask, one in zip(order + [0], pack(order + [0], count, video_query, video_key, video_value)):
        packs[mask] = one
    weight, cross_query, cross_key, cross_value, video_stream, own_audio = fetch(
        (out_weight, cross_query, cross_key, cross_value, video_stream), (audio_key, audio_value, audio_query)
    )
    for mask in order:
        packs[mask] = seq[mask](packs[mask])
    heads = [None] * count
    audios = [seq[mask](own_audio) if mask and (mask == 1 or mask % 2 == 0) else own_audio for mask in range(count)]
    done = [weight]
    for index, mask in enumerate(order + [0]):
        passed = [audios[m - 1] for m in range(3, count, 2)] if index == 1 else []
        heads[mask], *passed = attend([mask], order + [0], rows, packs, done, f"attend{index}", passed)
        for m, one in zip(range(3, count, 2), passed):
            audios[m] = seq[1](one)
        if mask:
            done = [heads[mask]]
    own_heads = list(heads)
    for mask in order:
        heads[mask] = seq[mask](heads[mask])

    groups = [(0, 1)] + [(1 << bit, 1 << bit) for bit in range(count.bit_length() - 1)]
    pieces = partials(
        groups, cross_key, cross_value, audios, [own_heads[1]]
    )
    others = list(range(2, tensor, 2))
    core = partner("tensor", tensor, 1)
    def halve(pieces, after):
        while len(pieces) > 2:
            mask = groups[len(pieces) - 1][0]
            other = seq[mask](pieces.pop())
            pieces = list(merge(pieces, other, False, after))
        return pieces

    pieces = list(pieces)
    chunks = 2 if share % 256 == 0 else 1
    got, after = [], pieces[:1]
    for part in range(chunks):
        sent = project(
            order + [0], heads, weight, share // chunks, {mask + 1: BF16 for mask in others}, "project_far", after,
            (part, chunks),
        )
        after = sent[:1]
        got.append([core(x) for x in sent])
    came = []
    for part in range(chunks):
        kept = project(
            order + [0], heads, weight, share // chunks, {mask: F32 for mask in others}, "project_kept", after,
            (part, chunks),
        )
        summed = [(mine + theirs.astype(F32)).astype(BF16) for mine, theirs in zip(kept, got[part])]
        came.append([partner("tensor", tensor, mask)(piece).astype(F32) for mask, piece in zip(others, summed)])
        after = summed[:1]
    own, near = project(order + [0], heads, weight, share, {1: BF16, 0: F32}, "project_near", summed)
    total = video_stream.astype(F32) + near + core(own).astype(F32)
    for index in range(len(others)):
        total = total + jnp.concatenate([one[index] for one in came], axis=1)
    video_next = total.astype(BF16)
    video_cross = crossed(cross_query, audios, summed)
    pieces = halve(pieces, summed)
    (audio_cross,) = merge(pieces[:1], seq[1](pieces[1]), True)
    return video_next, video_cross, audio_cross


def blank_state(query_rows, head_count):
    return (
        jnp.full((head_count, query_rows), -1e30, jnp.float32),
        jnp.zeros((head_count, query_rows), jnp.float32),
        jnp.zeros((head_count, query_rows, HD), jnp.float32),
    )


def absorb(carried, queries, keyset, values, head_count):
    running, row_sum, numerator = carried
    query_rows = queries.shape[0]
    key_rows = keyset.shape[0]
    factor = 1.0 / math.sqrt(HD)
    query_heads = queries.reshape(query_rows, head_count, HD)
    for offset in range(0, key_rows, 1024):
        width_keys = min(1024, key_rows - offset)
        key_block = keyset[offset : offset + width_keys].reshape(width_keys, head_count, HD)
        value_block = values[offset : offset + width_keys].reshape(width_keys, head_count, HD)
        scores = (
            jnp.einsum("qhd,khd->hqk", query_heads, key_block, preferred_element_type=jnp.float32)
            * factor
        )
        highest = jnp.maximum(running, jnp.max(scores, axis=2))
        raised = jnp.exp(scores - highest[:, :, None])
        shrink = jnp.exp(running - highest)
        row_sum = row_sum * shrink + jnp.sum(raised, axis=2)
        numerator = numerator * shrink[:, :, None] + jnp.einsum(
            "hqk,khd->hqd",
            raised.astype(jnp.bfloat16),
            value_block,
            preferred_element_type=jnp.float32,
        )
        running = highest
    return (running, row_sum, numerator)


def finish(carried, head_count):
    running, row_sum, numerator = carried
    result = numerator / row_sum[:, :, None]
    return result.transpose(1, 0, 2).reshape(result.shape[1], head_count * HD).astype(jnp.bfloat16)


def gathered(
    video_query,
    video_key,
    video_value,
    video_stream,
    out_weight,
    cross_query,
    audio_key,
    audio_value,
    audio_query,
    cross_key,
    cross_value,
):
    local_heads = video_query.shape[1] // HD
    query_rows = video_query.shape[0]
    pieces = (
        lax.all_gather(video_key, "seq", axis=0, tiled=True),
        lax.all_gather(video_value, "seq", axis=0, tiled=True),
    )
    carried_video = absorb(
        blank_state(query_rows, local_heads), video_query, pieces[0], pieces[1], local_heads
    )
    attended = finish(carried_video, local_heads)
    projected = jnp.dot(attended, out_weight, preferred_element_type=jnp.float32)
    summed = lax.psum_scatter(
        projected.astype(jnp.bfloat16), "tensor", scatter_dimension=1, tiled=True
    ).astype(jnp.float32)
    video_next = (video_stream.astype(jnp.float32) + summed).astype(jnp.bfloat16)
    cross_heads = cross_query.shape[1] // HD
    every_key, every_value = (
        lax.all_gather(audio_key, "seq", axis=0, tiled=True),
        lax.all_gather(audio_value, "seq", axis=0, tiled=True),
    )
    carried_audio = absorb(
        blank_state(cross_query.shape[0], cross_heads),
        cross_query,
        every_key,
        every_value,
        cross_heads,
    )
    video_cross = finish(carried_audio, cross_heads)
    pieces = (
        lax.all_gather(cross_key, "seq", axis=0, tiled=True),
        lax.all_gather(cross_value, "seq", axis=0, tiled=True),
    )
    carried_cross = absorb(
        blank_state(audio_query.shape[0], cross_heads),
        audio_query,
        pieces[0],
        pieces[1],
        cross_heads,
    )
    audio_cross = finish(carried_cross, cross_heads)
    return (video_next, video_cross, audio_cross)


def solution(mesh):
    count, tensor = mesh.shape["seq"], mesh.shape["tensor"]
    both = P(("groups", "seq"), "tensor")
    in_specs = (both,) * 4 + (P("tensor", None),) + (both,) * 6

    def local(*arrays):
        heads = arrays[0].shape[1] // HD
        powers = all(n > 1 and n & (n - 1) == 0 for n in (count, tensor))
        if powers and heads % count == 0 and arrays[6].shape[0] % 16 == 0:
            return exchanged(count, tensor, *arrays)
        return gathered(*arrays)

    return jax.shard_map(local, mesh=mesh, in_specs=in_specs, out_specs=(both,) * 3, check_vma=False)
```

```python
import functools
import math

import jax
import jax.numpy as jnp
from jax import lax
from jax.experimental import pallas as pl
from jax.experimental.pallas import tpu as pltpu
from jax.sharding import PartitionSpec as P


HD = 128
FACTOR = 1.0 / math.sqrt(HD)
LOG2E = math.log2(math.e)
BF16 = jnp.bfloat16
F32 = jnp.float32
MIB = 1 << 20
ANY = pl.BlockSpec(memory_space=pl.ANY)
HBM = pl.BlockSpec(memory_space=pltpu.HBM)
VM = pl.BlockSpec(memory_space=pltpu.VMEM)
WHOLE_VMEM = 62.75


COSTS = {"merge": 10000000000, "partials": 3000000000, "project_kept": 10000000000}


def call(kernel, name, shapes, ins, outs, operands, limit, scratch=(), flops=0):
    flops = COSTS.get(name, flops)
    return pl.pallas_call(
        kernel,
        out_shape=shapes,
        in_specs=ins,
        out_specs=outs,
        scratch_shapes=scratch,
        compiler_params=pltpu.CompilerParams(vmem_limit_bytes=int(limit * MIB)),
        cost_estimate=pl.CostEstimate(flops=flops, bytes_accessed=0, transcendentals=0),
        name=name,
    )(*operands)


def partner(axis, size, mask):
    return functools.partial(
        lax.ppermute, axis_name=axis, perm=[(i, i ^ mask) for i in range(size)]
    )


def nt(a, b):
    return lax.dot_general(a, b, (((1,), (1,)), ((), ())), preferred_element_type=F32)


def softmax_times(scores, value):
    highest = jnp.max(scores, axis=1, keepdims=True)
    raised = jnp.exp2(scores * (FACTOR * LOG2E) - highest * (FACTOR * LOG2E))
    total = jnp.sum(raised, axis=1, keepdims=True)
    numerator = jnp.dot(raised.astype(BF16), value, preferred_element_type=F32)
    return highest, total, numerator


def pack_kernel(masks, count, q, k, v, *rest):
    outs, sem = rest[:-1], rest[-1]
    rows, width = q.shape[0], q.shape[1] // count
    z = lax.axis_index("seq")
    copies = []
    for mask, out in zip(masks, outs):
        columns = pl.ds(pl.multiple_of(jnp.bitwise_xor(z, mask) * width, width), width)
        for position, source in enumerate((q, k, v)):
            target = out.at[pl.ds(position * rows, rows)]
            copies.append(pltpu.make_async_copy(source.at[:, columns], target, sem.at[len(copies)]))
            copies[-1].start()
    for one in copies:
        one.wait()


def pack(masks, count, q, k, v):
    shape = pltpu.VMEM((3 * q.shape[0], q.shape[1] // count), BF16)
    return call(
        functools.partial(pack_kernel, masks, count), "pack", [shape] * len(masks), [HBM] * 3, [VM] * len(masks),
        (q, k, v), WHOLE_VMEM, [pltpu.SemaphoreType.DMA((3 * len(masks),))],
    )


def attend_kernel(wanted, order, rows, carried, *refs):
    count = len(order)
    packs, outs = dict(zip(order, refs)), refs[-len(wanted) - carried :]
    for index in range(carried):
        refs[index - carried][...] = refs[count + index][...]
    for columns in range(0, packs[0].shape[1], HD):
        columns = slice(columns, columns + HD)
        key = jnp.concatenate([p[rows : 2 * rows, columns] for p in packs.values()], axis=0)
        value = jnp.concatenate([p[2 * rows : 3 * rows, columns] for p in packs.values()], axis=0)
        for mask, out in zip(wanted, outs):
            _, total, numerator = softmax_times(nt(packs[mask][:rows, columns], key), value)
            out[:, columns] = (numerator / total).astype(BF16)


def attend(wanted, order, rows, packs, after, name, carry=()):
    count, width = len(packs), packs[0].shape[1]
    return call(
        functools.partial(attend_kernel, wanted, order, rows, len(carry)), name,
        [jax.ShapeDtypeStruct((rows, width), BF16)] * len(wanted) + [jax.ShapeDtypeStruct(x.shape, x.dtype) for x in carry],
        [VM] * (count + len(carry)) + [ANY] * len(after), [VM] * (len(wanted) + len(carry)),
        (*(packs[mask] for mask in order), *carry, *after), 8,
        flops=4 * count * len(wanted) * rows * rows * width,
    )


def fetch_kernel(count, size, *refs):
    sources, refs = refs[:3], refs[3:]
    own_pack, refs = refs[-2], refs[:-2] + refs[-1:]
    pairs = list(zip(refs[:count], refs[count + 3 : 2 * count + 3]))
    own_audio, rows = refs[2 * count + 3], refs[count].shape[0]
    pairs += [(one, own_audio.at[pl.ds(kind * rows, rows)]) for kind, one in enumerate(refs[count : count + 3])]
    rows, width = sources[0].shape[0], sources[0].shape[1] // size
    columns = pl.ds(pl.multiple_of(lax.axis_index("seq") * width, width), width)
    pairs += [(one.at[:, columns], own_pack.at[pl.ds(kind * rows, rows)]) for kind, one in enumerate(sources)]
    copies = [pltpu.make_async_copy(*pair, refs[-1].at[i]) for i, pair in enumerate(pairs)]
    for one in copies:
        one.start()
    for one in copies:
        one.wait()


def fetch(size, video, arrays, audio):
    count = len(arrays)
    shapes = [pltpu.VMEM(x.shape, x.dtype) for x in arrays]
    shapes.append(pltpu.VMEM((3 * audio[0].shape[0], audio[0].shape[1]), BF16))
    shapes.append(pltpu.VMEM((3 * video[0].shape[0], video[0].shape[1] // size), BF16))
    return call(
        functools.partial(fetch_kernel, count, size), "fetch", shapes, [HBM] * (count + 6), [VM] * (count + 2),
        (*video, *arrays, *audio), 53, [pltpu.SemaphoreType.DMA((count + 6,))],
    )


def project_kernel(order, blocks, part, step, *refs):
    count = len(order)
    heads, w, lhs = refs[:count], refs[count], refs[-1]
    outs = refs[-1 - len(blocks) : -1]
    width = heads[0].shape[1]
    z = lax.axis_index("seq")
    t = lax.axis_index("tensor")
    for mask, one in zip(order, heads):
        owner = jnp.bitwise_xor(z, mask)
        lhs[:, pl.ds(pl.multiple_of(owner * width, width), width)] = one[...]
    part, parts = part
    for out, mask in zip(outs, blocks):
        share = out.shape[1]
        owner = jnp.bitwise_xor(t, mask)
        for start in range(0, share, step):
            columns = pl.ds(pl.multiple_of((owner * parts + part) * share + start, step), step)
            product = jnp.dot(lhs[...], w[:, columns], preferred_element_type=F32)
            out[:, start : start + step] = product.astype(out.dtype)


def project(order, heads, w, share, blocks, name, after=(), part=(0, 1)):
    count, rows = len(heads), heads[0].shape[0]
    return call(
        functools.partial(project_kernel, order, list(blocks), part, math.gcd(512, share)), name,
        [jax.ShapeDtypeStruct((rows, share), dtype) for dtype in blocks.values()],
        [VM] * (count + 1) + [ANY] * len(after), [VM] * len(blocks), (*(heads[mask] for mask in order), w, *after), 8,
        [pltpu.VMEM((rows, w.shape[0]), BF16)],
        flops=2 * rows * w.shape[0] * share * len(blocks),
    )


def stats_of(levels, rows):
    lane = lax.broadcasted_iota(jnp.int32, (rows, HD), 1)
    stats = jnp.zeros((rows, HD), F32)
    for head, level in enumerate(levels):
        for piece in range(3):
            rounded = level.astype(BF16).astype(F32)
            stats = jnp.where(lane == 3 * head + piece, rounded, stats)
            level = level - rounded
    return stats.astype(BF16)


def level_of(stats, head):
    return jnp.sum(stats[:, 3 * head : 3 * head + 3].astype(F32), axis=1, keepdims=True)


def audio_of(audios, kind, head):
    rows = audios[0].shape[0] // 3
    here = (slice(kind * rows, (kind + 1) * rows), slice(head * HD, (head + 1) * HD))
    return jnp.concatenate([one[here] for one in audios], axis=0)


def partial_kernel(groups, ck, cv, *refs):
    count = sum(size for _, size in groups)
    audios, parts = refs[:count], refs[-len(groups) :]
    arows = audios[0].shape[0] // 3
    heads = ck.shape[1] // HD
    levels = []
    for head in range(heads):
        columns = slice(head * HD, (head + 1) * HD)
        highest, total, numerator = softmax_times(nt(audio_of(audios, 2, head), ck[:, columns]), cv[:, columns])
        partial = (numerator / total).astype(BF16)
        levels.append(highest * (FACTOR * LOG2E) + jnp.log2(total))
        for (start, size), part in zip(groups, parts):
            part[:, columns] = partial[start * arows : (start + size) * arows]
    stats = stats_of(levels, count * arows)
    for (start, size), part in zip(groups, parts):
        part[:, heads * HD :] = stats[start * arows : (start + size) * arows]


def partials(groups, ck, cv, audios, after):
    count = len(audios)
    arows = audios[0].shape[0] // 3
    return call(
        functools.partial(partial_kernel, groups), "partials",
        [jax.ShapeDtypeStruct((size * arows, ck.shape[1] + HD), BF16) for _, size in groups],
        [VM] * (2 + count) + [ANY] * len(after), [VM] * len(groups),
        (ck, cv, *audios, *after), 8, flops=4 * count * arows * ck.size,
    )


def video_cross_kernel(count, cq, *refs):
    audios, out = refs[:count], refs[-1]
    for head in range(cq.shape[1] // HD):
        columns = slice(head * HD, (head + 1) * HD)
        _, total, numerator = softmax_times(nt(cq[:, columns], audio_of(audios, 0, head)), audio_of(audios, 1, head))
        out[:, columns] = (numerator / total).astype(BF16)


def crossed(cq, audios, after):
    count = len(audios)
    return call(
        functools.partial(video_cross_kernel, count), "video_cross",
        jax.ShapeDtypeStruct(cq.shape, BF16), [VM] * (1 + count) + [ANY] * len(after), VM,
        (cq, *audios, *after), 8, flops=4 * count * (audios[0].shape[0] // 3) * cq.size,
    )


def merge_kernel(last, pieces, *refs):
    mine, came, outs = refs[:pieces], refs[pieces], refs[-pieces:]
    at = 0
    for one, out in zip(mine, outs):
        rows, end = one.shape[0], one.shape[1] - HD
        two = came.at[at : at + rows]
        at += rows
        levels = []
        for head in range(end // HD):
            columns = slice(head * HD, (head + 1) * HD)
            left, right = level_of(one[:, end:], head), level_of(two[:, end:], head)
            highest = jnp.maximum(left, right)
            left, right = jnp.exp2(left - highest), jnp.exp2(right - highest)
            mixed = one[:, columns].astype(F32) * left + two[:, columns].astype(F32) * right
            out[:, columns] = (mixed / (left + right)).astype(BF16)
            levels.append(highest + jnp.log2(left + right))
        if not last:
            out[:, end:] = stats_of(levels, rows)


def merge(mine, came, last, after=()):
    cut = HD if last else 0
    shapes = [jax.ShapeDtypeStruct((x.shape[0], x.shape[1] - cut), BF16) for x in mine]
    return call(
        functools.partial(merge_kernel, last, len(mine)), "merge_last" if last else "merge", shapes,
        [VM] * (len(mine) + 1) + [ANY] * len(after), [VM] * len(mine), (*mine, came, *after), 4,
    )


def exchanged(count, tensor, video_query, video_key, video_value, video_stream, out_weight,
              cross_query, audio_key, audio_value, audio_query, cross_key, cross_value):
    rows = video_query.shape[0]
    share = out_weight.shape[1] // tensor
    seq = [partner("seq", count, mask) for mask in range(count)]
    order = list(range(count - 1, 0, -1))

    packs = [None] * count
    for mask, one in zip(order, pack(order, count, video_query, video_key, video_value)):
        packs[mask] = one
    weight, cross_query, cross_key, cross_value, video_stream, own_audio, packs[0] = fetch(
        count, (video_query, video_key, video_value), (out_weight, cross_query, cross_key, cross_value, video_stream), (audio_key, audio_value, audio_query)
    )
    for mask in order:
        packs[mask] = seq[mask](packs[mask])
    heads = [None] * count
    audios = [seq[mask](own_audio) if mask and (mask == 1 or mask % 2 == 0) else own_audio for mask in range(count)]
    done = [weight]
    for index, mask in enumerate(order + [0]):
        passed = [audios[m - 1] for m in range(3, count, 2)] if index == 1 else []
        heads[mask], *passed = attend([mask], order + [0], rows, packs, done, f"attend{index}", passed)
        for m, one in zip(range(3, count, 2), passed):
            audios[m] = seq[1](one)
        if mask:
            done = [heads[mask]]
    own_heads = list(heads)
    for mask in order:
        heads[mask] = seq[mask](heads[mask])

    groups = [(0, 1)] + [(1 << bit, 1 << bit) for bit in range(count.bit_length() - 1)]
    pieces = partials(
        groups, cross_key, cross_value, audios, [own_heads[1]]
    )
    others = list(range(2, tensor, 2))
    core = partner("tensor", tensor, 1)
    def halve(pieces, after):
        while len(pieces) > 2:
            mask = groups[len(pieces) - 1][0]
            other = seq[mask](pieces.pop())
            pieces = list(merge(pieces, other, False, after))
        return pieces

    pieces = list(pieces)
    chunks = 2 if share % 256 == 0 else 1
    got, after = [], pieces[:1]
    for part in range(chunks):
        sent = project(
            order + [0], heads, weight, share // chunks, {mask + 1: BF16 for mask in others}, "project_far", after,
            (part, chunks),
        )
        after = sent[:1]
        got.append([core(x) for x in sent])
    came = []
    for part in range(chunks):
        kept = project(
            order + [0], heads, weight, share // chunks, {mask: F32 for mask in others}, "project_kept", after,
            (part, chunks),
        )
        summed = [(mine + theirs.astype(F32)).astype(BF16) for mine, theirs in zip(kept, got[part])]
        came.append([partner("tensor", tensor, mask)(piece).astype(F32) for mask, piece in zip(others, summed)])
        after = summed[:1]
    own, near = project(order + [0], heads, weight, share, {1: BF16, 0: F32}, "project_near", summed)
    total = video_stream.astype(F32) + near + core(own).astype(F32)
    for index in range(len(others)):
        total = total + jnp.concatenate([one[index] for one in came], axis=1)
    video_next = total.astype(BF16)
    video_cross = crossed(cross_query, audios, summed)
    pieces = halve(pieces, summed)
    (audio_cross,) = merge(pieces[:1], seq[1](pieces[1]), True)
    return video_next, video_cross, audio_cross


def blank_state(query_rows, head_count):
    return (
        jnp.full((head_count, query_rows), -1e30, jnp.float32),
        jnp.zeros((head_count, query_rows), jnp.float32),
        jnp.zeros((head_count, query_rows, HD), jnp.float32),
    )


def absorb(carried, queries, keyset, values, head_count):
    running, row_sum, numerator = carried
    query_rows = queries.shape[0]
    key_rows = keyset.shape[0]
    factor = 1.0 / math.sqrt(HD)
    query_heads = queries.reshape(query_rows, head_count, HD)
    for offset in range(0, key_rows, 1024):
        width_keys = min(1024, key_rows - offset)
        key_block = keyset[offset : offset + width_keys].reshape(width_keys, head_count, HD)
        value_block = values[offset : offset + width_keys].reshape(width_keys, head_count, HD)
        scores = (
            jnp.einsum("qhd,khd->hqk", query_heads, key_block, preferred_element_type=jnp.float32)
            * factor
        )
        highest = jnp.maximum(running, jnp.max(scores, axis=2))
        raised = jnp.exp(scores - highest[:, :, None])
        shrink = jnp.exp(running - highest)
        row_sum = row_sum * shrink + jnp.sum(raised, axis=2)
        numerator = numerator * shrink[:, :, None] + jnp.einsum(
            "hqk,khd->hqd",
            raised.astype(jnp.bfloat16),
            value_block,
            preferred_element_type=jnp.float32,
        )
        running = highest
    return (running, row_sum, numerator)


def finish(carried, head_count):
    running, row_sum, numerator = carried
    result = numerator / row_sum[:, :, None]
    return result.transpose(1, 0, 2).reshape(result.shape[1], head_count * HD).astype(jnp.bfloat16)


def gathered(
    video_query,
    video_key,
    video_value,
    video_stream,
    out_weight,
    cross_query,
    audio_key,
    audio_value,
    audio_query,
    cross_key,
    cross_value,
):
    local_heads = video_query.shape[1] // HD
    query_rows = video_query.shape[0]
    pieces = (
        lax.all_gather(video_key, "seq", axis=0, tiled=True),
        lax.all_gather(video_value, "seq", axis=0, tiled=True),
    )
    carried_video = absorb(
        blank_state(query_rows, local_heads), video_query, pieces[0], pieces[1], local_heads
    )
    attended = finish(carried_video, local_heads)
    projected = jnp.dot(attended, out_weight, preferred_element_type=jnp.float32)
    summed = lax.psum_scatter(
        projected.astype(jnp.bfloat16), "tensor", scatter_dimension=1, tiled=True
    ).astype(jnp.float32)
    video_next = (video_stream.astype(jnp.float32) + summed).astype(jnp.bfloat16)
    cross_heads = cross_query.shape[1] // HD
    every_key, every_value = (
        lax.all_gather(audio_key, "seq", axis=0, tiled=True),
        lax.all_gather(audio_value, "seq", axis=0, tiled=True),
    )
    carried_audio = absorb(
        blank_state(cross_query.shape[0], cross_heads),
        cross_query,
        every_key,
        every_value,
        cross_heads,
    )
    video_cross = finish(carried_audio, cross_heads)
    pieces = (
        lax.all_gather(cross_key, "seq", axis=0, tiled=True),
        lax.all_gather(cross_value, "seq", axis=0, tiled=True),
    )
    carried_cross = absorb(
        blank_state(audio_query.shape[0], cross_heads),
        audio_query,
        pieces[0],
        pieces[1],
        cross_heads,
    )
    audio_cross = finish(carried_cross, cross_heads)
    return (video_next, video_cross, audio_cross)


def solution(mesh):
    count, tensor = mesh.shape["seq"], mesh.shape["tensor"]
    both = P(("groups", "seq"), "tensor")
    in_specs = (both,) * 4 + (P("tensor", None),) + (both,) * 6

    def local(*arrays):
        heads = arrays[0].shape[1] // HD
        powers = all(n > 1 and n & (n - 1) == 0 for n in (count, tensor))
        if powers and heads % count == 0 and arrays[6].shape[0] % 16 == 0:
            return exchanged(count, tensor, *arrays)
        return gathered(*arrays)

    return jax.shard_map(local, mesh=mesh, in_specs=in_specs, out_specs=(both,) * 3, check_vma=False)
```

```python
import functools
import math

import jax
import jax.numpy as jnp
from jax import lax
from jax.experimental import pallas as pl
from jax.experimental.pallas import tpu as pltpu
from jax.sharding import PartitionSpec as P


HD = 128
FACTOR = 1.0 / math.sqrt(HD)
LOG2E = math.log2(math.e)
BF16 = jnp.bfloat16
F32 = jnp.float32
MIB = 1 << 20
ANY = pl.BlockSpec(memory_space=pl.ANY)
HBM = pl.BlockSpec(memory_space=pltpu.HBM)
VM = pl.BlockSpec(memory_space=pltpu.VMEM)
WHOLE_VMEM = 62.75


COSTS = {"merge": 10000000000, "partials": 3000000000, "project_kept": 10000000000, "attend2": 1000000000}


def call(kernel, name, shapes, ins, outs, operands, limit, scratch=(), flops=0):
    flops = COSTS.get(name, flops)
    return pl.pallas_call(
        kernel,
        out_shape=shapes,
        in_specs=ins,
        out_specs=outs,
        scratch_shapes=scratch,
        compiler_params=pltpu.CompilerParams(vmem_limit_bytes=int(limit * MIB)),
        cost_estimate=pl.CostEstimate(flops=flops, bytes_accessed=0, transcendentals=0),
        name=name,
    )(*operands)


def partner(axis, size, mask):
    return functools.partial(
        lax.ppermute, axis_name=axis, perm=[(i, i ^ mask) for i in range(size)]
    )


def nt(a, b):
    return lax.dot_general(a, b, (((1,), (1,)), ((), ())), preferred_element_type=F32)


def softmax_times(scores, value):
    highest = jnp.max(scores, axis=1, keepdims=True)
    raised = jnp.exp2(scores * (FACTOR * LOG2E) - highest * (FACTOR * LOG2E))
    total = jnp.sum(raised, axis=1, keepdims=True)
    numerator = jnp.dot(raised.astype(BF16), value, preferred_element_type=F32)
    return highest, total, numerator


def pack_kernel(masks, count, q, k, v, *rest):
    outs, sem = rest[:-1], rest[-1]
    rows, width = q.shape[0], q.shape[1] // count
    z = lax.axis_index("seq")
    copies = []
    for mask, out in zip(masks, outs):
        columns = pl.ds(pl.multiple_of(jnp.bitwise_xor(z, mask) * width, width), width)
        for position, source in enumerate((q, k, v)):
            target = out.at[pl.ds(position * rows, rows)]
            copies.append(pltpu.make_async_copy(source.at[:, columns], target, sem.at[len(copies)]))
            copies[-1].start()
    for one in copies:
        one.wait()


def pack(masks, count, q, k, v):
    shape = pltpu.VMEM((3 * q.shape[0], q.shape[1] // count), BF16)
    return call(
        functools.partial(pack_kernel, masks, count), "pack", [shape] * len(masks), [HBM] * 3, [VM] * len(masks),
        (q, k, v), WHOLE_VMEM, [pltpu.SemaphoreType.DMA((3 * len(masks),))],
    )


def attend_kernel(wanted, order, rows, carried, *refs):
    count = len(order)
    packs, outs = dict(zip(order, refs)), refs[-len(wanted) - carried :]
    for index in range(carried):
        refs[index - carried][...] = refs[count + index][...]
    for columns in range(0, packs[0].shape[1], HD):
        columns = slice(columns, columns + HD)
        key = jnp.concatenate([p[rows : 2 * rows, columns] for p in packs.values()], axis=0)
        value = jnp.concatenate([p[2 * rows : 3 * rows, columns] for p in packs.values()], axis=0)
        for mask, out in zip(wanted, outs):
            _, total, numerator = softmax_times(nt(packs[mask][:rows, columns], key), value)
            out[:, columns] = (numerator / total).astype(BF16)


def attend(wanted, order, rows, packs, after, name, carry=()):
    count, width = len(packs), packs[0].shape[1]
    return call(
        functools.partial(attend_kernel, wanted, order, rows, len(carry)), name,
        [jax.ShapeDtypeStruct((rows, width), BF16)] * len(wanted) + [jax.ShapeDtypeStruct(x.shape, x.dtype) for x in carry],
        [VM] * (count + len(carry)) + [ANY] * len(after), [VM] * (len(wanted) + len(carry)),
        (*(packs[mask] for mask in order), *carry, *after), 8,
        flops=4 * count * len(wanted) * rows * rows * width,
    )


def fetch_kernel(count, size, *refs):
    sources, refs = refs[:3], refs[3:]
    own_pack, refs = refs[-2], refs[:-2] + refs[-1:]
    pairs = list(zip(refs[:count], refs[count + 3 : 2 * count + 3]))
    own_audio, rows = refs[2 * count + 3], refs[count].shape[0]
    pairs += [(one, own_audio.at[pl.ds(kind * rows, rows)]) for kind, one in enumerate(refs[count : count + 3])]
    rows, width = sources[0].shape[0], sources[0].shape[1] // size
    columns = pl.ds(pl.multiple_of(lax.axis_index("seq") * width, width), width)
    pairs += [(one.at[:, columns], own_pack.at[pl.ds(kind * rows, rows)]) for kind, one in enumerate(sources)]
    copies = [pltpu.make_async_copy(*pair, refs[-1].at[i]) for i, pair in enumerate(pairs)]
    for one in copies:
        one.start()
    for one in copies:
        one.wait()


def fetch(size, video, arrays, audio):
    count = len(arrays)
    shapes = [pltpu.VMEM(x.shape, x.dtype) for x in arrays]
    shapes.append(pltpu.VMEM((3 * audio[0].shape[0], audio[0].shape[1]), BF16))
    shapes.append(pltpu.VMEM((3 * video[0].shape[0], video[0].shape[1] // size), BF16))
    return call(
        functools.partial(fetch_kernel, count, size), "fetch", shapes, [HBM] * (count + 6), [VM] * (count + 2),
        (*video, *arrays, *audio), 53, [pltpu.SemaphoreType.DMA((count + 6,))],
    )


def project_kernel(order, blocks, part, step, *refs):
    count = len(order)
    heads, w, lhs = refs[:count], refs[count], refs[-1]
    outs = refs[-1 - len(blocks) : -1]
    width = heads[0].shape[1]
    z = lax.axis_index("seq")
    t = lax.axis_index("tensor")
    for mask, one in zip(order, heads):
        owner = jnp.bitwise_xor(z, mask)
        lhs[:, pl.ds(pl.multiple_of(owner * width, width), width)] = one[...]
    part, parts = part
    for out, mask in zip(outs, blocks):
        share = out.shape[1]
        owner = jnp.bitwise_xor(t, mask)
        for start in range(0, share, step):
            columns = pl.ds(pl.multiple_of((owner * parts + part) * share + start, step), step)
            product = jnp.dot(lhs[...], w[:, columns], preferred_element_type=F32)
            out[:, start : start + step] = product.astype(out.dtype)


def project(order, heads, w, share, blocks, name, after=(), part=(0, 1)):
    count, rows = len(heads), heads[0].shape[0]
    return call(
        functools.partial(project_kernel, order, list(blocks), part, math.gcd(512, share)), name,
        [jax.ShapeDtypeStruct((rows, share), dtype) for dtype in blocks.values()],
        [VM] * (count + 1) + [ANY] * len(after), [VM] * len(blocks), (*(heads[mask] for mask in order), w, *after), 8,
        [pltpu.VMEM((rows, w.shape[0]), BF16)],
        flops=2 * rows * w.shape[0] * share * len(blocks),
    )


def stats_of(levels, rows):
    lane = lax.broadcasted_iota(jnp.int32, (rows, HD), 1)
    stats = jnp.zeros((rows, HD), F32)
    for head, level in enumerate(levels):
        for piece in range(3):
            rounded = level.astype(BF16).astype(F32)
            stats = jnp.where(lane == 3 * head + piece, rounded, stats)
            level = level - rounded
    return stats.astype(BF16)


def level_of(stats, head):
    return jnp.sum(stats[:, 3 * head : 3 * head + 3].astype(F32), axis=1, keepdims=True)


def audio_of(audios, kind, head):
    rows = audios[0].shape[0] // 3
    here = (slice(kind * rows, (kind + 1) * rows), slice(head * HD, (head + 1) * HD))
    return jnp.concatenate([one[here] for one in audios], axis=0)


def partial_kernel(groups, ck, cv, *refs):
    count = sum(size for _, size in groups)
    audios, parts = refs[:count], refs[-len(groups) :]
    arows = audios[0].shape[0] // 3
    heads = ck.shape[1] // HD
    levels = []
    for head in range(heads):
        columns = slice(head * HD, (head + 1) * HD)
        highest, total, numerator = softmax_times(nt(audio_of(audios, 2, head), ck[:, columns]), cv[:, columns])
        partial = (numerator / total).astype(BF16)
        levels.append(highest * (FACTOR * LOG2E) + jnp.log2(total))
        for (start, size), part in zip(groups, parts):
            part[:, columns] = partial[start * arows : (start + size) * arows]
    stats = stats_of(levels, count * arows)
    for (start, size), part in zip(groups, parts):
        part[:, heads * HD :] = stats[start * arows : (start + size) * arows]


def partials(groups, ck, cv, audios, after):
    count = len(audios)
    arows = audios[0].shape[0] // 3
    return call(
        functools.partial(partial_kernel, groups), "partials",
        [jax.ShapeDtypeStruct((size * arows, ck.shape[1] + HD), BF16) for _, size in groups],
        [VM] * (2 + count) + [ANY] * len(after), [VM] * len(groups),
        (ck, cv, *audios, *after), 8, flops=4 * count * arows * ck.size,
    )


def video_cross_kernel(count, cq, *refs):
    audios, out = refs[:count], refs[-1]
    for head in range(cq.shape[1] // HD):
        columns = slice(head * HD, (head + 1) * HD)
        _, total, numerator = softmax_times(nt(cq[:, columns], audio_of(audios, 0, head)), audio_of(audios, 1, head))
        out[:, columns] = (numerator / total).astype(BF16)


def crossed(cq, audios, after):
    count = len(audios)
    return call(
        functools.partial(video_cross_kernel, count), "video_cross",
        jax.ShapeDtypeStruct(cq.shape, BF16), [VM] * (1 + count) + [ANY] * len(after), VM,
        (cq, *audios, *after), 8, flops=4 * count * (audios[0].shape[0] // 3) * cq.size,
    )


def merge_kernel(last, pieces, *refs):
    mine, came, outs = refs[:pieces], refs[pieces], refs[-pieces:]
    at = 0
    for one, out in zip(mine, outs):
        rows, end = one.shape[0], one.shape[1] - HD
        two = came.at[at : at + rows]
        at += rows
        levels = []
        for head in range(end // HD):
            columns = slice(head * HD, (head + 1) * HD)
            left, right = level_of(one[:, end:], head), level_of(two[:, end:], head)
            highest = jnp.maximum(left, right)
            left, right = jnp.exp2(left - highest), jnp.exp2(right - highest)
            mixed = one[:, columns].astype(F32) * left + two[:, columns].astype(F32) * right
            out[:, columns] = (mixed / (left + right)).astype(BF16)
            levels.append(highest + jnp.log2(left + right))
        if not last:
            out[:, end:] = stats_of(levels, rows)


def merge(mine, came, last, after=()):
    cut = HD if last else 0
    shapes = [jax.ShapeDtypeStruct((x.shape[0], x.shape[1] - cut), BF16) for x in mine]
    return call(
        functools.partial(merge_kernel, last, len(mine)), "merge_last" if last else "merge", shapes,
        [VM] * (len(mine) + 1) + [ANY] * len(after), [VM] * len(mine), (*mine, came, *after), 4,
    )


def exchanged(count, tensor, video_query, video_key, video_value, video_stream, out_weight,
              cross_query, audio_key, audio_value, audio_query, cross_key, cross_value):
    rows = video_query.shape[0]
    share = out_weight.shape[1] // tensor
    seq = [partner("seq", count, mask) for mask in range(count)]
    order = list(range(count - 1, 0, -1))

    packs = [None] * count
    for mask, one in zip(order, pack(order, count, video_query, video_key, video_value)):
        packs[mask] = one
    weight, cross_query, cross_key, cross_value, video_stream, own_audio, packs[0] = fetch(
        count, (video_query, video_key, video_value), (out_weight, cross_query, cross_key, cross_value, video_stream), (audio_key, audio_value, audio_query)
    )
    for mask in order:
        packs[mask] = seq[mask](packs[mask])
    heads = [None] * count
    audios = [seq[mask](own_audio) if mask and (mask == 1 or mask % 2 == 0) else own_audio for mask in range(count)]
    done = [weight]
    for index, mask in enumerate(order + [0]):
        passed = [audios[m - 1] for m in range(3, count, 2)] if index == 1 else []
        heads[mask], *passed = attend([mask], order + [0], rows, packs, done, f"attend{index}", passed)
        for m, one in zip(range(3, count, 2), passed):
            audios[m] = seq[1](one)
        if mask:
            done = [heads[mask]]
    own_heads = list(heads)
    for mask in order:
        heads[mask] = seq[mask](heads[mask])

    groups = [(0, 1)] + [(1 << bit, 1 << bit) for bit in range(count.bit_length() - 1)]
    pieces = partials(
        groups, cross_key, cross_value, audios, [own_heads[1]]
    )
    others = list(range(2, tensor, 2))
    core = partner("tensor", tensor, 1)
    def halve(pieces, after):
        while len(pieces) > 2:
            mask = groups[len(pieces) - 1][0]
            other = seq[mask](pieces.pop())
            pieces = list(merge(pieces, other, False, after))
        return pieces

    pieces = list(pieces)
    chunks = 2 if share % 256 == 0 else 1
    got, after = [], pieces[:1]
    for part in range(chunks):
        sent = project(
            order + [0], heads, weight, share // chunks, {mask + 1: BF16 for mask in others}, "project_far", after,
            (part, chunks),
        )
        after = sent[:1]
        got.append([core(x) for x in sent])
    came = []
    for part in range(chunks):
        kept = project(
            order + [0], heads, weight, share // chunks, {mask: F32 for mask in others}, "project_kept", after,
            (part, chunks),
        )
        summed = [(mine + theirs.astype(F32)).astype(BF16) for mine, theirs in zip(kept, got[part])]
        came.append([partner("tensor", tensor, mask)(piece).astype(F32) for mask, piece in zip(others, summed)])
        after = summed[:1]
    own, near = project(order + [0], heads, weight, share, {1: BF16, 0: F32}, "project_near", summed)
    total = video_stream.astype(F32) + near + core(own).astype(F32)
    for index in range(len(others)):
        total = total + jnp.concatenate([one[index] for one in came], axis=1)
    video_next = total.astype(BF16)
    video_cross = crossed(cross_query, audios, summed)
    pieces = halve(pieces, summed)
    (audio_cross,) = merge(pieces[:1], seq[1](pieces[1]), True)
    return video_next, video_cross, audio_cross


def blank_state(query_rows, head_count):
    return (
        jnp.full((head_count, query_rows), -1e30, jnp.float32),
        jnp.zeros((head_count, query_rows), jnp.float32),
        jnp.zeros((head_count, query_rows, HD), jnp.float32),
    )


def absorb(carried, queries, keyset, values, head_count):
    running, row_sum, numerator = carried
    query_rows = queries.shape[0]
    key_rows = keyset.shape[0]
    factor = 1.0 / math.sqrt(HD)
    query_heads = queries.reshape(query_rows, head_count, HD)
    for offset in range(0, key_rows, 1024):
        width_keys = min(1024, key_rows - offset)
        key_block = keyset[offset : offset + width_keys].reshape(width_keys, head_count, HD)
        value_block = values[offset : offset + width_keys].reshape(width_keys, head_count, HD)
        scores = (
            jnp.einsum("qhd,khd->hqk", query_heads, key_block, preferred_element_type=jnp.float32)
            * factor
        )
        highest = jnp.maximum(running, jnp.max(scores, axis=2))
        raised = jnp.exp(scores - highest[:, :, None])
        shrink = jnp.exp(running - highest)
        row_sum = row_sum * shrink + jnp.sum(raised, axis=2)
        numerator = numerator * shrink[:, :, None] + jnp.einsum(
            "hqk,khd->hqd",
            raised.astype(jnp.bfloat16),
            value_block,
            preferred_element_type=jnp.float32,
        )
        running = highest
    return (running, row_sum, numerator)


def finish(carried, head_count):
    running, row_sum, numerator = carried
    result = numerator / row_sum[:, :, None]
    return result.transpose(1, 0, 2).reshape(result.shape[1], head_count * HD).astype(jnp.bfloat16)


def gathered(
    video_query,
    video_key,
    video_value,
    video_stream,
    out_weight,
    cross_query,
    audio_key,
    audio_value,
    audio_query,
    cross_key,
    cross_value,
):
    local_heads = video_query.shape[1] // HD
    query_rows = video_query.shape[0]
    pieces = (
        lax.all_gather(video_key, "seq", axis=0, tiled=True),
        lax.all_gather(video_value, "seq", axis=0, tiled=True),
    )
    carried_video = absorb(
        blank_state(query_rows, local_heads), video_query, pieces[0], pieces[1], local_heads
    )
    attended = finish(carried_video, local_heads)
    projected = jnp.dot(attended, out_weight, preferred_element_type=jnp.float32)
    summed = lax.psum_scatter(
        projected.astype(jnp.bfloat16), "tensor", scatter_dimension=1, tiled=True
    ).astype(jnp.float32)
    video_next = (video_stream.astype(jnp.float32) + summed).astype(jnp.bfloat16)
    cross_heads = cross_query.shape[1] // HD
    every_key, every_value = (
        lax.all_gather(audio_key, "seq", axis=0, tiled=True),
        lax.all_gather(audio_value, "seq", axis=0, tiled=True),
    )
    carried_audio = absorb(
        blank_state(cross_query.shape[0], cross_heads),
        cross_query,
        every_key,
        every_value,
        cross_heads,
    )
    video_cross = finish(carried_audio, cross_heads)
    pieces = (
        lax.all_gather(cross_key, "seq", axis=0, tiled=True),
        lax.all_gather(cross_value, "seq", axis=0, tiled=True),
    )
    carried_cross = absorb(
        blank_state(audio_query.shape[0], cross_heads),
        audio_query,
        pieces[0],
        pieces[1],
        cross_heads,
    )
    audio_cross = finish(carried_cross, cross_heads)
    return (video_next, video_cross, audio_cross)


def solution(mesh):
    count, tensor = mesh.shape["seq"], mesh.shape["tensor"]
    both = P(("groups", "seq"), "tensor")
    in_specs = (both,) * 4 + (P("tensor", None),) + (both,) * 6

    def local(*arrays):
        heads = arrays[0].shape[1] // HD
        powers = all(n > 1 and n & (n - 1) == 0 for n in (count, tensor))
        if powers and heads % count == 0 and arrays[6].shape[0] % 16 == 0:
            return exchanged(count, tensor, *arrays)
        return gathered(*arrays)

    return jax.shard_map(local, mesh=mesh, in_specs=in_specs, out_specs=(both,) * 3, check_vma=False)
```
